512 devices in a mesh: gx: 32 (over z, core), gy: 16 (over y, x).
Axes of the slice: x: 4, y: 4, z: 16, core: 2. Of those that a mesh axis runs over, the one named last changes fastest.
Arguments:
- source: float32 [32, 4096, 2048], P(None, 'gx', 'gy'), may hold values from -6 to 6
- stretch_index: int32 [2048], replicated, may hold values from 0 to 8, as said below
- mode_index: int32 [512], replicated, may hold values from 0 to 2047, as said below
Outputs:
- pressure_modes: float32 [2, 32, 512, 2048], P(None, None, 'gx', 'gy')
The draws below stay inside these ranges and needn't reach their ends.
Inputs may be any that keep to these rules, and one draw needn't show every extreme that they name: `stretch_index`: 0 at both walls and 8 at the two centre cells; neighbouring cells differ by at most one. `mode_index`: 512 distinct wavenumbers; 0 and 2047 are always among them.
All inputs are finite; a program needn't handle non-finite values.
Results may differ from the reference program's by a relative error of at most 0.0017.
Values sent between devices are 32-bit elements; how exact they have to be, the bound alone decides.
No kernel may reach another device: no remote copies, remote signals or barrier semaphores. Data moves between devices by JAX's collectives and lax.ppermute only.
A program may use at most 64 MiB of HBM per device.

```python
import math
import jax
import jax.numpy as jnp
from jax import lax

NX = 4096
NY = 2048
NZ = 32
KM = 512


def draw_stretch_index(key, part):
    key = jax.random.fold_in(key, 11)
    half_rows = NY // 2 - 1
    cells = jnp.arange(NY, dtype=jnp.int32)
    distance = jnp.minimum(cells, NY - 1 - cells)
    offset = jax.random.randint(key, (NY,), 0, half_rows // 2 + 1)
    offset = jnp.where((distance == 0) | (distance == half_rows), 0, offset)
    levels = (8 * distance + offset) // half_rows
    return jnp.clip(levels, 0, 8).astype(jnp.int32)


def draw_mode_index(key, part):
    key = jax.random.fold_in(key, 7)
    half_modes = NX // 2
    inner_modes = jax.random.permutation(key, half_modes - 2) + 1
    chosen = jnp.concatenate([jnp.array([0, half_modes - 1], jnp.int32), inner_modes[:KM - 2].astype(jnp.int32)])
    ordering = jax.random.permutation(jax.random.fold_in(key, 1), KM)
    return chosen[ordering]


def steps_of(key, dims, split, least, largest):
    def one(position, parts):
        draws = jax.random.uniform(jax.random.fold_in(jax.random.fold_in(key, 6), position), (parts,), jnp.float32, least / len(split), largest / len(split))
        return jnp.repeat(jnp.exp(draws), dims[position] // parts).reshape((-1,) + (1,) * (len(dims) - position - 1))

    loudness = one(*split[0])
    for cut in split[1:]:
        loudness = loudness * one(*cut)
    return loudness


def noise(own_key, shape, spread, most, cuts=(), kind=jnp.bfloat16):
    entries = jax.random.normal(own_key, shape, jnp.float32) * spread
    if len(cuts) > 0:
        entries = steps_of(own_key, shape, cuts, -0.22, 0.18) * entries
    return jnp.clip(entries, min=-most, max=most).astype(kind)


def setup_inputs(seed: int = 0) -> dict:
    key_list = jax.random.split(jax.random.key(seed), 4)
    source = noise(key_list[0], (NZ, NX, NY), 1.0, 6.0, ((1, 32), (2, 16)), jnp.float32)
    stretch_index = draw_stretch_index(jax.random.fold_in(key_list[3], 71), 0)
    mode_index = draw_mode_index(jax.random.fold_in(key_list[3], 71), 0)
    return {"source": source, "stretch_index": stretch_index, "mode_index": mode_index}


def spacing_bands(stretch_index):
    spacing = 0.25 * jnp.exp2(0.25 * stretch_index.astype(jnp.float32))
    faces = 0.5 * (spacing[:-1] + spacing[1:])
    zeros_one = jnp.zeros((1,), jnp.float32)
    lower_band = jnp.concatenate([zeros_one, 1.0 / (spacing[1:] * faces)])
    upper_band = jnp.concatenate([1.0 / (spacing[:-1] * faces), zeros_one])
    return (lower_band, upper_band)

def shift_terms(mode_values, plane_count, stream_length):
    stream_wave = mode_values.astype(jnp.float32) * (2.0 * math.pi / stream_length)
    span_wave = 0.04 * (jnp.arange(plane_count, dtype=jnp.float32) + 1.0)
    return span_wave[:, None] * span_wave[:, None] + stream_wave[None, :] * stream_wave[None, :]

def reference(source, stretch_index, mode_index):
    lower_band, upper_band = spacing_bands(stretch_index)
    terms = shift_terms(mode_index, NZ, NX)

    def per_plane(inputs):
        plane_field, plane_terms = inputs
        spectra = jnp.fft.rfft(plane_field, axis=0)[mode_index] / jnp.sqrt(jnp.float32(NX))
        right_side = jnp.stack([spectra.real.astype(jnp.float32), spectra.imag.astype(jnp.float32)], -1)
        diagonal = lower_band + upper_band + plane_terms[:, None]
        below_band = jnp.broadcast_to(-lower_band, diagonal.shape)
        above_band = jnp.broadcast_to(-upper_band, diagonal.shape)
        solved = lax.linalg.tridiagonal_solve(below_band, diagonal, above_band, right_side)
        return jnp.moveaxis(solved, -1, 0)
    stacked = lax.map(per_plane, (source, terms))
    return jnp.moveaxis(stacked, 0, 1)
```

```python
import functools
import math

import jax
import jax.numpy as jnp
from jax import lax
from jax.experimental import pallas as pl
from jax.experimental.pallas import tpu as pltpu
from jax.sharding import PartitionSpec as P

F32 = jnp.float32
BF16 = jnp.bfloat16
VMEM = pl.BlockSpec(memory_space=pltpu.VMEM)
SMEM = pl.BlockSpec(memory_space=pltpu.SMEM)
PARAMS = pltpu.CompilerParams(vmem_limit_bytes=48 * 1024 * 1024)


def spacing_bands(stretch_index):
    spacing = 0.25 * jnp.exp2(0.25 * stretch_index.astype(F32))
    faces = 0.5 * (spacing[:-1] + spacing[1:])
    zeros_one = jnp.zeros((1,), F32)
    lower_band = jnp.concatenate([zeros_one, 1.0 / (spacing[1:] * faces)])
    upper_band = jnp.concatenate([1.0 / (spacing[:-1] * faces), zeros_one])
    return (lower_band, upper_band)


def halves(values):
    high = values.astype(BF16)
    low = (values - high.astype(F32)).astype(BF16)
    return high, low


def table_kernel(length, starts_ref, modes_ref, high_ref, low_ref):
    quarter = length // 4
    mode_column = modes_ref[...]
    for side in range(2):
        place = starts_ref[side] + lax.broadcasted_iota(jnp.int32, (1, 128), 1)
        phase = (mode_column * place) & (length - 1)
        turn = (phase + quarter // 2) // quarter
        angle = (phase - turn * quarter).astype(F32) * (2.0 * math.pi / length)
        square = angle * angle
        sine = angle * (
            1.0
            + square
            * (-1.0 / 6 + square * (1.0 / 120 + square * (-1.0 / 5040 + square * (1.0 / 362880))))
        )
        cosine = 1.0 + square * (
            -0.5 + square * (1.0 / 24 + square * (-1.0 / 720 + square * (1.0 / 40320)))
        )
        odd = (turn & 1) == 1
        real = jnp.where(odd, sine, cosine)
        imag = jnp.where(odd, cosine, sine)
        scale = 1.0 / math.sqrt(length)
        real = jnp.where(((turn + 1) & 2) == 2, -scale, scale) * real
        imag = jnp.where((turn & 2) == 2, scale, -scale) * imag
        columns = pl.ds(side * 128, 128)
        for part, values in enumerate((real, imag)):
            high, low = halves(values)
            high_ref[:, part, :, columns] = high.reshape(-1, 16, 128)
            low_ref[:, part, :, columns] = low.reshape(-1, 16, 128)


def spectrum_kernel(core_ref, high_ref, low_ref, own_ref, got_ref, out_ref):
    del core_ref
    field = jnp.concatenate(
        [
            jnp.concatenate([own_ref[0], own_ref[1]], 1),
            jnp.concatenate([got_ref[0], got_ref[1]], 1),
        ],
        0,
    )
    field_high, field_low = halves(field)
    chips = out_ref.shape[0]
    step = 4
    for first in range(0, chips, step):
        rows = pl.ds(first * 64, step * 64)
        high = high_ref[rows, :]
        total = jnp.dot(high, field_high, preferred_element_type=F32)
        total += jnp.dot(high, field_low, preferred_element_type=F32)
        total += jnp.dot(low_ref[rows, :], field_high, preferred_element_type=F32)
        for plane in range(2):
            piece = total[:, plane * 128 : (plane + 1) * 128]
            out_ref[pl.ds(first, step), :, plane, :, :] = piece.reshape(step, 2, 32, 128)


def factor_kernel(
    info_ref,
    low_ref,
    up_ref,
    modes_ref,
    ratio_ref,
    inverse_ref,
    back_ref,
    left_ref,
    right_ref,
    carry_ref,
    corner,
):
    core = info_ref[0]
    block = info_ref[1]
    rows = 128
    blocks = carry_ref.shape[1] // 1
    sublane = lax.broadcasted_iota(jnp.int32, (8, 128), 0)
    lane = lax.broadcasted_iota(jnp.int32, (8, 128), 1)
    half = jnp.where(sublane < 4, core, 1 - core)
    plane = 16 * half + 4 * (sublane & 3) + lane // 32
    span_wave = 0.04 * (plane.astype(F32) + 1.0)
    stream_wave = modes_ref[...].astype(F32) * (2.0 * math.pi / 4096)
    shift = span_wave * span_wave + stream_wave * stream_wave

    group = 8
    for first in range(0, blocks, group):
        state = []
        for b in range(first, first + group):
            low, up = low_ref[b * rows], up_ref[b * rows]
            inverse = 1.0 / (low + up + shift)
            state.append((inverse, jnp.ones_like(shift), up * inverse, inverse))

        def forward(j, state):
            later = []
            for k in range(group):
                at = (first + k) * rows + j
                low, up, before = low_ref[at], up_ref[at], up_ref[at - 1]
                inverse, chain, product, corner_sum = state[k]
                ratio = low * inverse
                inverse = 1.0 / (low + up + shift - ratio * before)
                chain = chain * ratio
                corner_sum = corner_sum + product * (chain * inverse)
                later.append((inverse, chain, product * (up * inverse), corner_sum))
            return tuple(later)

        state = lax.fori_loop(1, rows, forward, tuple(state))
        for k in range(group):
            b = first + k
            inverse, chain, product, corner_sum = state[k]
            low, up = low_ref[b * rows], up_ref[b * rows + rows - 1]
            corner[0, b] = low * corner_sum
            corner[1, b] = low * (chain * inverse)
            corner[2, b] = product
            corner[3, b] = up * inverse

    reach = jnp.zeros_like(shift)
    for b in range(blocks):
        left_first, left_last = corner[0, b], corner[1, b]
        right_first, right_last = corner[2, b], corner[3, b]
        gain = 1.0 / (1.0 - left_first * reach)
        carry_ref[0, b] = left_last * gain
        carry_ref[1, b] = left_last * reach * gain
        carry_ref[2, b] = gain
        carry_ref[3, b] = gain * left_first
        carry_ref[4, b] = gain * right_first
        carry_ref[5, b] = reach
        reach = right_last + left_last * reach * gain * right_first

    start = block * rows
    low, up = low_ref[start], up_ref[start]
    inverse = 1.0 / (low + up + shift)
    ratio_ref[0] = jnp.zeros_like(shift)
    inverse_ref[0] = inverse
    back_ref[0] = up * inverse
    chain = low * jnp.ones_like(shift)
    left_ref[0] = chain

    def own_forward(j, state):
        inverse, chain = state
        low, up, before = low_ref[start + j], up_ref[start + j], up_ref[start + j - 1]
        ratio = low * inverse
        inverse = 1.0 / (low + up + shift - ratio * before)
        chain = chain * ratio
        ratio_ref[j] = ratio
        inverse_ref[j] = inverse
        back_ref[j] = up * inverse
        left_ref[j] = chain
        return (inverse, chain)

    lax.fori_loop(1, rows, own_forward, (inverse, chain))

    def own_backward(i, state):
        left, right = state
        j = rows - 1 - i
        back = back_ref[j]
        left = left_ref[j] * inverse_ref[j] + back * left
        right = back * right
        left_ref[j] = left
        right_ref[j] = right
        return (left, right)

    lax.fori_loop(
        0, rows, own_backward, (jnp.zeros_like(shift), jnp.ones_like(shift)), unroll=4
    )


def sweep_kernel(
    core_ref, kept_ref, got_ref, ratio_ref, inverse_ref, back_ref, solved_ref, ends_ref
):
    del core_ref
    for k in range(8):
        if k < 4:
            piece = kept_ref[0, pl.ds(128 * k, 128), :]
        else:
            piece = got_ref[pl.ds(128 * (k - 4), 128), :]
        solved_ref[pl.ds(k, 128, stride=8), :] = piece.T

    def forward(j, value):
        at = pl.ds(pl.multiple_of(j * 8, 8), 8)
        value = solved_ref[at, :] + ratio_ref[j] * value
        solved_ref[at, :] = value
        return value

    zero = jnp.zeros((8, 128), F32)
    lax.fori_loop(0, 128, forward, zero, unroll=16)

    def backward(i, value):
        j = 127 - i
        at = pl.ds(pl.multiple_of(j * 8, 8), 8)
        value = solved_ref[at, :] * inverse_ref[j] + back_ref[j] * value
        solved_ref[at, :] = value
        return value

    ends_ref[0] = lax.fori_loop(0, 128, backward, zero, unroll=16)
    ends_ref[1] = solved_ref[pl.ds(127 * 8, 8), :]


def combine_kernel(
    info_ref, ends_ref, carry_ref, solved_ref, left_ref, right_ref, out_ref, total, sums, firsts
):
    core = info_ref[0]
    block = info_ref[1]
    blocks = ends_ref.shape[0]
    before = jnp.zeros((8, 128), F32)
    for b in range(blocks):
        sums[b] = before
        first, last = ends_ref[b, 0], ends_ref[b, 1]
        before = last + carry_ref[1, b] * first + carry_ref[0, b] * before
    after = jnp.zeros((8, 128), F32)
    for b in reversed(range(blocks)):
        firsts[b + 1] = after
        base = carry_ref[2, b] * ends_ref[b, 0] + carry_ref[3, b] * sums[b]
        after = base + carry_ref[4, b] * after
    firsts[0] = after
    from_left = sums[block] + carry_ref[5, block] * firsts[block]
    from_right = firsts[block + 1]

    def join(j, unused):
        at = pl.ds(pl.multiple_of(j * 8, 8), 8)
        total[at, :] = solved_ref[at, :] + from_left * left_ref[j] + from_right * right_ref[j]
        return unused

    lax.fori_loop(0, 128, join, 0, unroll=16)
    for k in range(8):
        piece = total[pl.ds(k, 128, stride=8), :].T
        half = core if k < 4 else 1 - core
        for z in range(4):
            for part in range(2):
                rows = piece[z * 32 + part * 16 : z * 32 + part * 16 + 16]
                out_ref[part, 16 * half + 4 * (k % 4) + z] = rows


def local(source, stretch_index, mode_index):
    gx_count = lax.axis_size("gx")
    gy_count = lax.axis_size("gy")
    planes, stream_rows, wall_rows = source.shape
    length = stream_rows * gx_count
    gx_index = lax.axis_index("gx")
    gy_index = lax.axis_index("gy")
    core = gx_index % 2
    half_planes = planes // 2
    partner = [(i, i ^ 1) for i in range(gx_count)]
    chips = gx_count // 2

    core_info = core.astype(jnp.int32)[None]
    info = jnp.stack([core, gy_index]).astype(jnp.int32)

    sent = lax.dynamic_slice_in_dim(source, (1 - core) * half_planes, half_planes)
    got = lax.ppermute(sent, "gx", partner)

    starts = jnp.stack([gx_index * stream_rows, (gx_index ^ 1) * stream_rows]).astype(jnp.int32)
    table_shape = jax.ShapeDtypeStruct((gx_count, 2, 16, 256), BF16)
    table_high, table_low = pl.pallas_call(
        functools.partial(table_kernel, length),
        out_shape=(table_shape, table_shape),
        in_specs=[SMEM, VMEM],
        out_specs=(VMEM, VMEM),
        compiler_params=PARAMS,
        name="tables",
    )(starts, mode_index[:, None])
    table_high = table_high.reshape(gx_count * 32, 256)
    table_low = table_low.reshape(gx_count * 32, 256)

    table_spec = pl.BlockSpec((gx_count * 32, 256), lambda i, c: (0, 0))
    partial_sums = pl.pallas_call(
        spectrum_kernel,
        out_shape=jax.ShapeDtypeStruct((chips, 2, half_planes, 32, wall_rows), F32),
        grid_spec=pltpu.PrefetchScalarGridSpec(
            num_scalar_prefetch=1,
            grid=(half_planes // 2,),
            in_specs=[
                table_spec,
                table_spec,
                pl.BlockSpec(
                    (2, stream_rows, wall_rows), lambda i, c: (c[0] * (half_planes // 2) + i, 0, 0)
                ),
                pl.BlockSpec((2, stream_rows, wall_rows), lambda i, c: (i, 0, 0)),
            ],
            out_specs=pl.BlockSpec((chips, 2, 2, 32, wall_rows), lambda i, c: (0, 0, i, 0, 0)),
        ),
        compiler_params=PARAMS,
        name="spectrum",
    )(core_info, table_high, table_low, source, got)

    rings = [[2 * chip + c for chip in range(chips)] for c in range(2)]
    partial_sums = partial_sums.reshape(chips * half_planes * 64, wall_rows)
    summed = lax.psum_scatter(
        partial_sums, "gx", scatter_dimension=0, axis_index_groups=rings, tiled=True
    ).reshape(2, half_planes * 32, wall_rows)

    lower_all, upper_all = spacing_bands(stretch_index)
    own_modes = lax.dynamic_slice_in_dim(mode_index, gx_index * 16, 16)
    own_modes = jnp.tile(own_modes, 8)[None, :]
    column = jax.ShapeDtypeStruct((wall_rows, 8, 128), F32)
    carry_shape = jax.ShapeDtypeStruct((6, gy_count, 8, 128), F32)
    ratio, inverse, back, left, right, carry = pl.pallas_call(
        factor_kernel,
        out_shape=(column,) * 5 + (carry_shape,),
        in_specs=[SMEM, SMEM, SMEM, VMEM],
        out_specs=(VMEM,) * 6,
        scratch_shapes=[pltpu.VMEM((4, gy_count, 8, 128), F32)],
        compiler_params=PARAMS,
        name="factors",
    )(info, lower_all, upper_all, own_modes)

    given = lax.dynamic_slice_in_dim(summed, 1 - core, 1)[0]
    taken = lax.ppermute(given, "gx", partner)

    whole = pl.BlockSpec((wall_rows, 8, 128), lambda i, c: (0, 0, 0))
    solved, ends = pl.pallas_call(
        sweep_kernel,
        out_shape=(
            jax.ShapeDtypeStruct((wall_rows * 8, 128), F32),
            jax.ShapeDtypeStruct((2, 8, 128), F32),
        ),
        grid_spec=pltpu.PrefetchScalarGridSpec(
            num_scalar_prefetch=1,
            grid=(1,),
            in_specs=[
                pl.BlockSpec((1, half_planes * 32, wall_rows), lambda i, c: (c[0], 0, 0)),
                pl.BlockSpec((half_planes * 32, wall_rows), lambda i, c: (0, 0)),
                whole,
                whole,
                whole,
            ],
            out_specs=(
                pl.BlockSpec((wall_rows * 8, 128), lambda i, c: (0, 0)),
                pl.BlockSpec((2, 8, 128), lambda i, c: (0, 0, 0)),
            ),
        ),
        compiler_params=PARAMS,
        name="sweeps",
    )(core_info, summed, taken, ratio, inverse, back)

    copies = jnp.broadcast_to(ends[None], (gy_count, 2, 8, 128))
    all_ends = lax.all_to_all(copies, "gy", split_axis=0, concat_axis=0, tiled=True)

    return pl.pallas_call(
        combine_kernel,
        out_shape=jax.ShapeDtypeStruct((2, planes, 16, wall_rows), F32),
        in_specs=[SMEM] + [VMEM] * 5,
        out_specs=VMEM,
        scratch_shapes=[
            pltpu.VMEM((wall_rows * 8, 128), F32),
            pltpu.VMEM((gy_count, 8, 128), F32),
            pltpu.VMEM((gy_count + 1, 8, 128), F32),
        ],
        compiler_params=PARAMS,
        name="combine",
    )(info, all_ends, carry, solved, left, right)


def solution(mesh):
    in_specs = (P(None, "gx", "gy"), P(), P())
    out_specs = P(None, None, "gx", "gy")
    return jax.shard_map(local, mesh=mesh, in_specs=in_specs, out_specs=out_specs, check_vma=False)
```

```python
import functools
import math

import jax
import jax.numpy as jnp
from jax import lax
from jax.experimental import pallas as pl
from jax.experimental.pallas import tpu as pltpu
from jax.sharding import PartitionSpec as P

F32 = jnp.float32
BF16 = jnp.bfloat16
VMEM = pl.BlockSpec(memory_space=pltpu.VMEM)
SMEM = pl.BlockSpec(memory_space=pltpu.SMEM)
PARAMS = pltpu.CompilerParams(vmem_limit_bytes=48 * 1024 * 1024)


def spacing_bands(stretch_index):
    spacing = 0.25 * jnp.exp2(0.25 * stretch_index.astype(F32))
    faces = 0.5 * (spacing[:-1] + spacing[1:])
    zeros_one = jnp.zeros((1,), F32)
    lower_band = jnp.concatenate([zeros_one, 1.0 / (spacing[1:] * faces)])
    upper_band = jnp.concatenate([1.0 / (spacing[:-1] * faces), zeros_one])
    return (lower_band, upper_band)


def halves(values):
    high = values.astype(BF16)
    low = (values - high.astype(F32)).astype(BF16)
    return high, low


def wave(phase, length):
    quarter = length // 4
    phase = phase & (length - 1)
    turn = (phase + quarter // 2) // quarter
    angle = (phase - turn * quarter).astype(F32) * (2.0 * math.pi / length)
    square = angle * angle
    sine = angle * (
        1.0
        + square
        * (-1.0 / 6 + square * (1.0 / 120 + square * (-1.0 / 5040 + square * (1.0 / 362880))))
    )
    cosine = 1.0 + square * (
        -0.5 + square * (1.0 / 24 + square * (-1.0 / 720 + square * (1.0 / 40320)))
    )
    odd = (turn & 1) == 1
    real = jnp.where(odd, sine, cosine)
    imag = jnp.where(odd, cosine, sine)
    real = jnp.where(((turn + 1) & 2) == 2, -real, real)
    imag = jnp.where((turn & 2) == 2, -imag, imag)
    return real, imag


def table_kernel(length, starts_ref, modes_ref, high_ref, low_ref):
    mode_column = modes_ref[...]
    for side in range(2):
        place = starts_ref[side] + lax.broadcasted_iota(jnp.int32, (1, 128), 1)
        real, imag = wave(mode_column * place, length)
        scale = 1.0 / math.sqrt(length)
        columns = pl.ds(side * 128, 128)
        for part, values in enumerate((real * scale, imag * -scale)):
            high, low = halves(values)
            high_ref[:, part, :, columns] = high.reshape(-1, 16, 128)
            low_ref[:, part, :, columns] = low.reshape(-1, 16, 128)


def spectrum_kernel(high_ref, low_ref, own_ref, got_ref, out_ref):
    count = own_ref.shape[0]
    for plane in range(0, count, 2):
        field = jnp.concatenate(
            [
                jnp.concatenate([own_ref[plane], own_ref[plane + 1]], 1),
                jnp.concatenate([got_ref[plane], got_ref[plane + 1]], 1),
            ],
            0,
        )
        field_high, field_low = halves(field)
        step = 8
        for first in range(0, out_ref.shape[0], step):
            rows = pl.ds(first * 32, step * 32)
            high = high_ref[rows, :]
            total = jnp.dot(high, field_high, preferred_element_type=F32)
            total += jnp.dot(high, field_low, preferred_element_type=F32)
            total += jnp.dot(low_ref[rows, :], field_high, preferred_element_type=F32)
            for k in range(2):
                piece = total[:, k * 128 : (k + 1) * 128]
                out_ref[pl.ds(first, step), plane + k] = piece.reshape(step, 32, 128)


def shift_of(plane, modes):
    span_wave = 0.04 * (plane.astype(F32) + 1.0)
    stream_wave = modes.astype(F32) * (2.0 * math.pi / 4096)
    return span_wave * span_wave + stream_wave * stream_wave


def carry_kernel(low_ref, up_ref, modes_ref, carry_ref, corner):
    rows = 128
    blocks = carry_ref.shape[1]
    sublane = lax.broadcasted_iota(jnp.int32, (8, 128), 0)
    lane = lax.broadcasted_iota(jnp.int32, (8, 128), 1)
    shift = shift_of(4 * sublane + lane // 32, modes_ref[...])

    group = 8
    for first in range(0, blocks, group):
        state = []
        for b in range(first, first + group):
            low, up = low_ref[b * rows], up_ref[b * rows]
            inverse = 1.0 / (low + up + shift)
            state.append((inverse, jnp.ones_like(shift), up * inverse, inverse))

        def forward(j, state):
            later = []
            for k in range(group):
                at = (first + k) * rows + j
                low, up, before = low_ref[at], up_ref[at], up_ref[at - 1]
                inverse, chain, product, corner_sum = state[k]
                ratio = low * inverse
                inverse = 1.0 / (low + up + shift - ratio * before)
                chain = chain * ratio
                corner_sum = corner_sum + product * (chain * inverse)
                later.append((inverse, chain, product * (up * inverse), corner_sum))
            return tuple(later)

        state = lax.fori_loop(1, rows, forward, tuple(state))
        for k in range(group):
            b = first + k
            inverse, chain, product, corner_sum = state[k]
            low, up = low_ref[b * rows], up_ref[b * rows + rows - 1]
            corner[0, b] = low * corner_sum
            corner[1, b] = low * (chain * inverse)
            corner[2, b] = product
            corner[3, b] = up * inverse

    reach = jnp.zeros_like(shift)
    for b in range(blocks):
        left_first, left_last = corner[0, b], corner[1, b]
        right_first, right_last = corner[2, b], corner[3, b]
        gain = 1.0 / (1.0 - left_first * reach)
        carry_ref[0, b] = left_last * gain
        carry_ref[1, b] = left_last * reach * gain
        carry_ref[2, b] = gain
        carry_ref[3, b] = gain * left_first
        carry_ref[4, b] = gain * right_first
        carry_ref[5, b] = reach
        reach = right_last + left_last * reach * gain * right_first


def weights_kernel(info_ref, low_ref, up_ref, modes_ref, first_ref, last_ref):
    rows = 128
    groups = first_ref.shape[0]
    start = info_ref[1] * rows
    end = start + rows - 1
    sublane = lax.broadcasted_iota(jnp.int32, (8, 128), 0)
    shifts = [shift_of(4 * w + sublane // 2, modes_ref[...]) for w in range(groups)]

    state = []
    for w in range(groups):
        down = 1.0 / (low_ref[start] + up_ref[start] + shifts[w])
        rising = 1.0 / (low_ref[end] + up_ref[end] + shifts[w])
        last_ref[w, pl.ds(0, 8), :] = down
        first_ref[w, pl.ds(8 * (rows - 1), 8), :] = rising
        state += [down, rising]

    def eliminate(i, state):
        j, k = start + i, end - i
        later = []
        for w in range(groups):
            down, rising = state[2 * w], state[2 * w + 1]
            down = 1.0 / (low_ref[j] + up_ref[j] + shifts[w] - (low_ref[j] * down) * up_ref[j - 1])
            last_ref[w, pl.ds(pl.multiple_of(8 * i, 8), 8), :] = down
            rising = 1.0 / (
                low_ref[k] + up_ref[k] + shifts[w] - (up_ref[k] * rising) * low_ref[k + 1]
            )
            first_ref[w, pl.ds(pl.multiple_of(8 * (rows - 1 - i), 8), 8), :] = rising
            later += [down, rising]
        return tuple(later)

    state = lax.fori_loop(1, rows, eliminate, tuple(state))

    def spread(i, state):
        j = rows - 1 - i
        later = []
        for w in range(groups):
            last, first = state[2 * w], state[2 * w + 1]
            at = pl.ds(pl.multiple_of(8 * j, 8), 8)
            last = last * (low_ref[start + j + 1] * last_ref[w, at, :])
            last_ref[w, at, :] = last
            at = pl.ds(pl.multiple_of(8 * i, 8), 8)
            first = first * (up_ref[start + i - 1] * first_ref[w, at, :])
            first_ref[w, at, :] = first
            later += [last, first]
        return tuple(later)

    lax.fori_loop(1, rows, spread, state)


def ends_kernel(sums_ref, first_ref, last_ref, ends_ref):
    for row in range(8):
        plane, half = row // 2, row % 2
        at = pl.ds(row, 128, stride=8)
        first, last = first_ref[0, at, :], last_ref[0, at, :]
        for part in range(2):
            values = sums_ref[pl.ds(8 * half, 8), plane, pl.ds(16 * part, 16), :]
            values = values.reshape(128, 128).T
            ends_ref[0, part, pl.ds(row, 1), :] = jnp.sum(values * first, 0, keepdims=True)
            ends_ref[1, part, pl.ds(row, 1), :] = jnp.sum(values * last, 0, keepdims=True)


def interface_kernel(info_ref, ends_ref, carry_ref, edge_ref, sums, firsts):
    block = info_ref[1]
    blocks = ends_ref.shape[0]
    before = jnp.zeros((8, 128), F32)
    for b in range(blocks):
        sums[b] = before
        before = ends_ref[b, 1] + carry_ref[1, b] * ends_ref[b, 0] + carry_ref[0, b] * before
    after = jnp.zeros((8, 128), F32)
    for b in reversed(range(blocks)):
        firsts[b + 1] = after
        base = carry_ref[2, b] * ends_ref[b, 0] + carry_ref[3, b] * sums[b]
        after = base + carry_ref[4, b] * after
    firsts[0] = after
    edge_ref[0] = sums[block] + carry_ref[5, block] * firsts[block]
    edge_ref[1] = firsts[block + 1]


def own_factor_kernel(info_ref, low_ref, up_ref, modes_ref, ratio_ref, inverse_ref, back_ref):
    rows = 128
    sublane = lax.broadcasted_iota(jnp.int32, (8, 128), 0)
    lane = lax.broadcasted_iota(jnp.int32, (8, 128), 1)
    shift = shift_of(4 * sublane + lane // 32, modes_ref[...])
    start = info_ref[1] * rows
    low, up = low_ref[start], up_ref[start]
    inverse = 1.0 / (low + up + shift)
    ratio_ref[0] = jnp.zeros_like(shift)
    inverse_ref[0] = inverse
    back_ref[0] = up * inverse

    def forward(j, inverse):
        low, up, before = low_ref[start + j], up_ref[start + j], up_ref[start + j - 1]
        ratio = low * inverse
        inverse = 1.0 / (low + up + shift - ratio * before)
        ratio_ref[j] = ratio
        inverse_ref[j] = inverse
        back_ref[j] = up * inverse
        return inverse

    lax.fori_loop(1, rows, forward, inverse)


def solve_kernel(
    info_ref, low_ref, up_ref, sums_ref, edge_ref, ratio_ref, inverse_ref, back_ref, out_ref, work
):
    rows = 128
    start = info_ref[1] * rows
    for k in range(8):
        work[pl.ds(k, rows, stride=8), :] = sums_ref[pl.ds(128 * k, 128), :].T
    work[pl.ds(0, 8), :] += low_ref[start] * edge_ref[0]
    work[pl.ds((rows - 1) * 8, 8), :] += up_ref[start + rows - 1] * edge_ref[1]

    def forward(j, value):
        at = pl.ds(pl.multiple_of(j * 8, 8), 8)
        value = work[at, :] + ratio_ref[j] * value
        work[at, :] = value
        return value

    zero = jnp.zeros((8, 128), F32)
    lax.fori_loop(0, rows, forward, zero, unroll=16)

    def backward(i, value):
        j = rows - 1 - i
        at = pl.ds(pl.multiple_of(j * 8, 8), 8)
        value = work[at, :] * inverse_ref[j] + back_ref[j] * value
        work[at, :] = value
        return value

    lax.fori_loop(0, rows, backward, zero, unroll=16)
    for k in range(8):
        piece = work[pl.ds(k, rows, stride=8), :].T
        for z in range(4):
            for part in range(2):
                at = z * 32 + part * 16
                out_ref[part, 4 * k + z] = piece[at : at + 16]


def local(source, stretch_index, mode_index):
    gx_count = lax.axis_size("gx")
    gy_count = lax.axis_size("gy")
    planes, stream_rows, wall_rows = source.shape
    length = stream_rows * gx_count
    gx_index = lax.axis_index("gx")
    gy_index = lax.axis_index("gy")
    core = gx_index % 2
    chips = gx_count // 2
    info = jnp.stack([core, gy_index]).astype(jnp.int32)

    got = lax.ppermute(source, "gx", [(i, i ^ 1) for i in range(gx_count)])
    core_modes = lax.dynamic_slice_in_dim(mode_index.reshape(chips, 2, 16), core, 1, 1)
    core_modes = core_modes.reshape(chips * 16)

    starts = jnp.stack([gx_index * stream_rows, (gx_index ^ 1) * stream_rows]).astype(jnp.int32)
    table_shape = jax.ShapeDtypeStruct((chips, 2, 16, 256), BF16)
    table_high, table_low = pl.pallas_call(
        functools.partial(table_kernel, length),
        out_shape=(table_shape, table_shape),
        in_specs=[SMEM, VMEM],
        out_specs=(VMEM, VMEM),
        compiler_params=PARAMS,
        name="tables",
    )(starts, core_modes[:, None])

    some = 4
    table_spec = pl.BlockSpec((chips * 32, 256), lambda i: (0, 0))
    field_spec = pl.BlockSpec((some, stream_rows, wall_rows), lambda i: (i, 0, 0))
    partial_spec = pl.BlockSpec((chips, some, 32, wall_rows), lambda i: (0, i, 0, 0))
    partial_sums = pl.pallas_call(
        spectrum_kernel,
        out_shape=jax.ShapeDtypeStruct((chips, planes, 32, wall_rows), F32),
        grid=(planes // some,),
        in_specs=[table_spec, table_spec, field_spec, field_spec],
        out_specs=partial_spec,
        compiler_params=PARAMS,
        name="spectrum",
    )(
        table_high.reshape(chips * 32, 256),
        table_low.reshape(chips * 32, 256),
        source,
        got,
    )

    rings = [[2 * chip + c for chip in range(chips)] for c in range(2)]
    summed = lax.psum_scatter(
        partial_sums.reshape(chips * planes * 32, wall_rows),
        "gx",
        scatter_dimension=0,
        axis_index_groups=rings,
        tiled=True,
    )

    lower_all, upper_all = spacing_bands(stretch_index)
    groups = planes // 4
    weights = jax.ShapeDtypeStruct((groups, wall_rows * 8, 128), F32)
    first_row, last_row = pl.pallas_call(
        weights_kernel,
        out_shape=(weights, weights),
        in_specs=[SMEM, SMEM, SMEM, VMEM],
        out_specs=(VMEM, VMEM),
        compiler_params=PARAMS,
        name="weights",
    )(info, lower_all, upper_all, jnp.tile(core_modes.reshape(2, 128), (4, 1)))
    weight_spec = pl.BlockSpec((1, wall_rows * 8, 128), lambda i: (i, 0, 0))
    ends = pl.pallas_call(
        ends_kernel,
        out_shape=jax.ShapeDtypeStruct((2, 2, groups * 8, 128), F32),
        grid=(groups,),
        in_specs=[partial_spec, weight_spec, weight_spec],
        out_specs=pl.BlockSpec((2, 2, 8, 128), lambda i: (0, 0, i, 0)),
        compiler_params=PARAMS,
        name="ends",
    )(partial_sums, first_row, last_row)
    ends = ends.reshape(2, 2, planes, 2, 8, 16).transpose(3, 4, 0, 2, 1, 5)
    ends = ends.reshape(chips, 2, 8, 128)
    ends = lax.all_to_all(
        ends, "gx", split_axis=0, concat_axis=0, axis_index_groups=rings, tiled=True
    ).sum(0)
    copies = jnp.broadcast_to(ends[None], (gy_count, 2, 8, 128))
    all_ends = lax.all_to_all(copies, "gy", split_axis=0, concat_axis=0, tiled=True)

    own_modes = lax.dynamic_slice_in_dim(mode_index, gx_index * 16, 16)
    own_modes = jnp.tile(own_modes, 8)[None, :]
    carry = pl.pallas_call(
        carry_kernel,
        out_shape=jax.ShapeDtypeStruct((6, gy_count, 8, 128), F32),
        in_specs=[SMEM, SMEM, VMEM],
        out_specs=VMEM,
        scratch_shapes=[pltpu.VMEM((4, gy_count, 8, 128), F32)],
        compiler_params=PARAMS,
        name="carry",
    )(lower_all, upper_all, own_modes)
    edges = pl.pallas_call(
        interface_kernel,
        out_shape=jax.ShapeDtypeStruct((2, 8, 128), F32),
        in_specs=[SMEM, VMEM, VMEM],
        out_specs=VMEM,
        scratch_shapes=[
            pltpu.VMEM((gy_count, 8, 128), F32),
            pltpu.VMEM((gy_count + 1, 8, 128), F32),
        ],
        compiler_params=PARAMS,
        name="interfaces",
    )(info, all_ends, carry)

    column = jax.ShapeDtypeStruct((wall_rows, 8, 128), F32)
    ratio, inverse, back = pl.pallas_call(
        own_factor_kernel,
        out_shape=(column,) * 3,
        in_specs=[SMEM, SMEM, SMEM, VMEM],
        out_specs=(VMEM,) * 3,
        compiler_params=PARAMS,
        name="own_factors",
    )(info, lower_all, upper_all, own_modes)

    summed, edges, ratio = lax.optimization_barrier((summed, edges, ratio))
    return pl.pallas_call(
        solve_kernel,
        out_shape=jax.ShapeDtypeStruct((2, planes, 16, wall_rows), F32),
        in_specs=[SMEM] * 3 + [VMEM] * 5,
        out_specs=VMEM,
        scratch_shapes=[pltpu.VMEM((wall_rows * 8, 128), F32)],
        compiler_params=PARAMS,
        name="solve",
    )(info, lower_all, upper_all, summed, edges, ratio, inverse, back)


def solution(mesh):
    in_specs = (P(None, "gx", "gy"), P(), P())
    out_specs = P(None, None, "gx", "gy")
    return jax.shard_map(local, mesh=mesh, in_specs=in_specs, out_specs=out_specs, check_vma=False)
```

```python
import functools
import math

import jax
import jax.numpy as jnp
from jax import lax
from jax.experimental import pallas as pl
from jax.experimental.pallas import tpu as pltpu
from jax.sharding import PartitionSpec as P

F32 = jnp.float32
BF16 = jnp.bfloat16
VMEM = pl.BlockSpec(memory_space=pltpu.VMEM)
SMEM = pl.BlockSpec(memory_space=pltpu.SMEM)
PARAMS = pltpu.CompilerParams(vmem_limit_bytes=48 * 1024 * 1024)


def spacing_bands(stretch_index):
    spacing = 0.25 * jnp.exp2(0.25 * stretch_index.astype(F32))
    faces = 0.5 * (spacing[:-1] + spacing[1:])
    zeros_one = jnp.zeros((1,), F32)
    lower_band = jnp.concatenate([zeros_one, 1.0 / (spacing[1:] * faces)])
    upper_band = jnp.concatenate([1.0 / (spacing[:-1] * faces), zeros_one])
    return (lower_band, upper_band)


def halves(values):
    high = values.astype(BF16)
    low = (values - high.astype(F32)).astype(BF16)
    return high, low


def wave(phase, length):
    quarter = length // 4
    phase = phase & (length - 1)
    turn = (phase + quarter // 2) // quarter
    angle = (phase - turn * quarter).astype(F32) * (2.0 * math.pi / length)
    square = angle * angle
    sine = angle * (
        1.0
        + square
        * (-1.0 / 6 + square * (1.0 / 120 + square * (-1.0 / 5040 + square * (1.0 / 362880))))
    )
    cosine = 1.0 + square * (
        -0.5 + square * (1.0 / 24 + square * (-1.0 / 720 + square * (1.0 / 40320)))
    )
    odd = (turn & 1) == 1
    real = jnp.where(odd, sine, cosine)
    imag = jnp.where(odd, cosine, sine)
    real = jnp.where(((turn + 1) & 2) == 2, -real, real)
    imag = jnp.where((turn & 2) == 2, -imag, imag)
    return real, imag


def table_kernel(
    length, info_ref, modes_ref, own_ref, high_ref, low_ref, own_high_ref, own_low_ref, own, sems
):
    core, index = info_ref[0], info_ref[2]
    steps = sems.shape[0]
    some = own_ref.shape[0] // steps
    groups = [pl.ds(some * g, some) for g in range(steps)]
    loads = [
        pltpu.make_async_copy(own_ref.at[groups[g]], own.at[groups[g]], sems.at[g])
        for g in range(steps)
    ]
    for load in loads:
        load.start()
    chips = high_ref.shape[0]
    mode_column = jnp.concatenate([modes_ref[2 * chip + core] for chip in range(chips)], 0)
    for side in range(2):
        start = 128 * (index ^ side)
        place = start + lax.broadcasted_iota(jnp.int32, (1, 128), 1)
        real, imag = wave(mode_column * place, length)
        scale = 1.0 / math.sqrt(length)
        columns = pl.ds(side * 128, 128)
        for part, values in enumerate((real * scale, imag * -scale)):
            high, low = halves(values)
            high_ref[:, part, :, columns] = high.reshape(-1, 16, 128)
            low_ref[:, part, :, columns] = low.reshape(-1, 16, 128)
    for g in range(steps):
        loads[g].wait()
        own_high_ref[groups[g]], own_low_ref[groups[g]] = halves(own[groups[g]])


def spectrum_kernel(
    high_ref, low_ref, own_high_ref, own_low_ref, got_ref, out_ref, sums, out_sems
):
    slots, chips, some = sums.shape[:3]
    steps = got_ref.shape[0] // some
    stores = [
        pltpu.make_async_copy(
            sums.at[g % slots], out_ref.at[:, pl.ds(some * g, some)], out_sems.at[g % slots]
        )
        for g in range(steps)
    ]

    def beside(ref, plane):
        return jnp.concatenate([ref[plane], ref[plane + 1]], 1)

    for g in range(steps):
        if g >= slots:
            stores[g - slots].wait()
        for pair in range(0, some, 2):
            plane = some * g + pair
            got_high, got_low = halves(beside(got_ref, plane))
            field_high = jnp.concatenate([beside(own_high_ref, plane), got_high], 0)
            field_low = jnp.concatenate([beside(own_low_ref, plane), got_low], 0)
            step = 8
            for first in range(0, chips, step):
                rows = pl.ds(first * 32, step * 32)
                high = high_ref[rows, :]
                total = jnp.dot(high, field_high, preferred_element_type=F32)
                total += jnp.dot(high, field_low, preferred_element_type=F32)
                total += jnp.dot(low_ref[rows, :], field_high, preferred_element_type=F32)
                for k in range(2):
                    piece = total[:, k * 128 : (k + 1) * 128].reshape(step, 32, 128)
                    sums[g % slots, pl.ds(first, step), pair + k] = piece
        stores[g].start()
    for g in range(max(0, steps - slots), steps):
        stores[g].wait()


def shift_of(plane, modes):
    span_wave = 0.04 * (plane.astype(F32) + 1.0)
    stream_wave = modes.astype(F32) * (2.0 * math.pi / 4096)
    return span_wave * span_wave + stream_wave * stream_wave


def carry_kernel(low_ref, up_ref, modes_ref, carry_ref, corner):
    rows = 128
    blocks = carry_ref.shape[1]
    sublane = lax.broadcasted_iota(jnp.int32, (8, 128), 0)
    lane = lax.broadcasted_iota(jnp.int32, (8, 128), 1)
    shift = shift_of(4 * sublane + lane // 32, modes_ref[...])

    group = 8
    for first in range(0, blocks, group):
        state = []
        for b in range(first, first + group):
            low, up = low_ref[b * rows], up_ref[b * rows]
            inverse = 1.0 / (low + up + shift)
            state.append((inverse, jnp.ones_like(shift), up * inverse, inverse))

        def forward(j, state):
            later = []
            for k in range(group):
                at = (first + k) * rows + j
                low, up, before = low_ref[at], up_ref[at], up_ref[at - 1]
                inverse, chain, product, corner_sum = state[k]
                ratio = low * inverse
                inverse = 1.0 / (low + up + shift - ratio * before)
                chain = chain * ratio
                corner_sum = corner_sum + product * (chain * inverse)
                later.append((inverse, chain, product * (up * inverse), corner_sum))
            return tuple(later)

        state = lax.fori_loop(1, rows, forward, tuple(state))
        for k in range(group):
            b = first + k
            inverse, chain, product, corner_sum = state[k]
            low, up = low_ref[b * rows], up_ref[b * rows + rows - 1]
            corner[0, b] = low * corner_sum
            corner[1, b] = low * (chain * inverse)
            corner[2, b] = product
            corner[3, b] = up * inverse

    reach = jnp.zeros_like(shift)
    for b in range(blocks):
        left_first, left_last = corner[0, b], corner[1, b]
        right_first, right_last = corner[2, b], corner[3, b]
        gain = 1.0 / (1.0 - left_first * reach)
        carry_ref[0, b] = left_last * gain
        carry_ref[1, b] = left_last * reach * gain
        carry_ref[2, b] = gain
        carry_ref[3, b] = gain * left_first
        carry_ref[4, b] = gain * right_first
        carry_ref[5, b] = reach
        reach = right_last + left_last * reach * gain * right_first


def weights_kernel(info_ref, low_ref, up_ref, modes_ref, first_ref, last_ref):
    rows = 128
    groups = first_ref.shape[0]
    start = info_ref[1] * rows
    end = start + rows - 1
    sublane = lax.broadcasted_iota(jnp.int32, (8, 128), 0)
    shifts = [shift_of(4 * w + sublane // 2, modes_ref[...]) for w in range(groups)]

    state = []
    for w in range(groups):
        down = 1.0 / (low_ref[start] + up_ref[start] + shifts[w])
        rising = 1.0 / (low_ref[end] + up_ref[end] + shifts[w])
        last_ref[w, pl.ds(0, 8), :] = down
        first_ref[w, pl.ds(8 * (rows - 1), 8), :] = rising
        state += [down, rising]

    def eliminate(i, state):
        j, k = start + i, end - i
        later = []
        for w in range(groups):
            down, rising = state[2 * w], state[2 * w + 1]
            down = 1.0 / (low_ref[j] + up_ref[j] + shifts[w] - (low_ref[j] * down) * up_ref[j - 1])
            last_ref[w, pl.ds(pl.multiple_of(8 * i, 8), 8), :] = down
            rising = 1.0 / (
                low_ref[k] + up_ref[k] + shifts[w] - (up_ref[k] * rising) * low_ref[k + 1]
            )
            first_ref[w, pl.ds(pl.multiple_of(8 * (rows - 1 - i), 8), 8), :] = rising
            later += [down, rising]
        return tuple(later)

    state = lax.fori_loop(1, rows, eliminate, tuple(state))

    def spread(i, state):
        j = rows - 1 - i
        later = []
        for w in range(groups):
            last, first = state[2 * w], state[2 * w + 1]
            at = pl.ds(pl.multiple_of(8 * j, 8), 8)
            last = last * (low_ref[start + j + 1] * last_ref[w, at, :])
            last_ref[w, at, :] = last
            at = pl.ds(pl.multiple_of(8 * i, 8), 8)
            first = first * (up_ref[start + i - 1] * first_ref[w, at, :])
            first_ref[w, at, :] = first
            later += [last, first]
        return tuple(later)

    lax.fori_loop(1, rows, spread, state)


def ends_kernel(sums_ref, first_ref, last_ref, ends_ref):
    for row in range(8):
        plane, half = row // 2, row % 2
        at = pl.ds(row, 128, stride=8)
        first, last = first_ref[0, at, :], last_ref[0, at, :]
        for part in range(2):
            values = sums_ref[pl.ds(8 * half, 8), plane, pl.ds(16 * part, 16), :]
            values = values.reshape(128, 128).T
            ends_ref[0, part, pl.ds(row, 1), :] = jnp.sum(values * first, 0, keepdims=True)
            ends_ref[1, part, pl.ds(row, 1), :] = jnp.sum(values * last, 0, keepdims=True)


def interface_kernel(info_ref, ends_ref, carry_ref, edge_ref, sums, firsts):
    block = info_ref[1]
    blocks = ends_ref.shape[0]
    before = jnp.zeros((8, 128), F32)
    for b in range(blocks):
        sums[b] = before
        before = ends_ref[b, 1] + carry_ref[1, b] * ends_ref[b, 0] + carry_ref[0, b] * before
    after = jnp.zeros((8, 128), F32)
    for b in reversed(range(blocks)):
        firsts[b + 1] = after
        base = carry_ref[2, b] * ends_ref[b, 0] + carry_ref[3, b] * sums[b]
        after = base + carry_ref[4, b] * after
    firsts[0] = after
    edge_ref[0] = sums[block] + carry_ref[5, block] * firsts[block]
    edge_ref[1] = firsts[block + 1]


def own_factor_kernel(info_ref, low_ref, up_ref, modes_ref, ratio_ref, inverse_ref, back_ref):
    rows = 128
    half = rows // 2
    sublane = lax.broadcasted_iota(jnp.int32, (8, 128), 0)
    lane = lax.broadcasted_iota(jnp.int32, (8, 128), 1)
    shift = shift_of(4 * sublane + lane // 32, modes_ref[...])
    start = info_ref[1] * rows
    end = start + rows - 1

    def pivot(at):
        return low_ref[at] + up_ref[at] + shift

    down = 1.0 / pivot(start)
    rising = 1.0 / pivot(end)
    ratio_ref[0] = jnp.zeros_like(shift)
    ratio_ref[rows - 1] = jnp.zeros_like(shift)
    inverse_ref[0] = down
    inverse_ref[rows - 1] = rising
    back_ref[0] = up_ref[start] * down
    back_ref[rows - 1] = low_ref[end] * rising

    def eliminate(i, state):
        down, rising = state
        j, k = start + i, end - i
        ratio = low_ref[j] * down
        down = 1.0 / (pivot(j) - ratio * up_ref[j - 1])
        ratio_ref[i] = ratio
        inverse_ref[i] = down
        back_ref[i] = up_ref[j] * down
        ratio = up_ref[k] * rising
        rising = 1.0 / (pivot(k) - ratio * low_ref[k + 1])
        ratio_ref[rows - 1 - i] = ratio
        inverse_ref[rows - 1 - i] = rising
        back_ref[rows - 1 - i] = low_ref[k] * rising
        return (down, rising)

    down, rising = lax.fori_loop(1, half, eliminate, (down, rising))
    across = 1.0 / (1.0 - back_ref[half - 1] * back_ref[half])
    inverse_ref[half - 1] = down * across
    inverse_ref[half] = rising * across


def solve_kernel(
    info_ref,
    low_ref,
    up_ref,
    sums_ref,
    edge_ref,
    ratio_ref,
    inverse_ref,
    back_ref,
    out_ref,
    work,
):
    rows = 128
    half = rows // 2
    start = info_ref[1] * rows
    for k in range(8):
        work[pl.ds(k, rows, stride=8), :] = sums_ref[pl.ds(rows * k, rows), :].T

    def row(j):
        return pl.ds(pl.multiple_of(j * 8, 8), 8)

    upper = work[row(0), :] + low_ref[start] * edge_ref[0]
    lower = work[row(rows - 1), :] + up_ref[start + rows - 1] * edge_ref[1]
    work[row(0), :] = upper
    work[row(rows - 1), :] = lower

    def inwards(j, state):
        upper, lower = state
        k = rows - 1 - j
        upper = work[row(j), :] + ratio_ref[j] * upper
        work[row(j), :] = upper
        lower = work[row(k), :] + ratio_ref[k] * lower
        work[row(k), :] = lower
        return (upper, lower)

    upper, lower = lax.fori_loop(1, half, inwards, (upper, lower), unroll=63)

    first = upper * inverse_ref[half - 1]
    second = lower * inverse_ref[half]
    upper = first + back_ref[half - 1] * second
    lower = second + back_ref[half] * first
    work[row(half - 1), :] = upper
    work[row(half), :] = lower

    def outwards(i, state):
        upper, lower = state
        j = half - 1 - i
        k = half + i
        upper = work[row(j), :] * inverse_ref[j] + back_ref[j] * upper
        work[row(j), :] = upper
        lower = work[row(k), :] * inverse_ref[k] + back_ref[k] * lower
        work[row(k), :] = lower
        return (upper, lower)

    lax.fori_loop(1, half, outwards, (upper, lower), unroll=63)
    for k in range(8):
        piece = work[pl.ds(k, rows, stride=8), :].T
        for z in range(4):
            for part in range(2):
                at = z * 32 + part * 16
                out_ref[part, 4 * k + z] = piece[at : at + 16]


def local(source, stretch_index, mode_index):
    gx_count = lax.axis_size("gx")
    gy_count = lax.axis_size("gy")
    planes, stream_rows, wall_rows = source.shape
    length = stream_rows * gx_count
    gx_index = lax.axis_index("gx")
    gy_index = lax.axis_index("gy")
    core = gx_index % 2
    chips = gx_count // 2
    info = jnp.stack([core, gy_index, gx_index]).astype(jnp.int32)

    got = lax.ppermute(source, "gx", [(i, i ^ 1) for i in range(gx_count)])
    hbm = pl.BlockSpec(memory_space=pltpu.HBM)
    source = pltpu.with_memory_space_constraint(source, pltpu.HBM)
    table_shape = jax.ShapeDtypeStruct((chips, 2, 16, 256), BF16)
    own_shape = jax.ShapeDtypeStruct(source.shape, BF16)
    table_high, table_low, own_high, own_low = pl.pallas_call(
        functools.partial(table_kernel, length),
        out_shape=(table_shape, table_shape, own_shape, own_shape),
        in_specs=[SMEM, VMEM, hbm],
        out_specs=(VMEM,) * 4,
        scratch_shapes=[pltpu.VMEM(source.shape, F32), pltpu.SemaphoreType.DMA((4,))],
        compiler_params=PARAMS,
        name="tables",
    )(info, mode_index.reshape(gx_count, 16, 1), source)

    some = 8
    slots = 3
    partial_sums = pl.pallas_call(
        spectrum_kernel,
        out_shape=jax.ShapeDtypeStruct((chips, planes, 32, wall_rows), F32),
        in_specs=[VMEM] * 5,
        out_specs=hbm,
        scratch_shapes=[
            pltpu.VMEM((slots, chips, some, 32, wall_rows), F32),
            pltpu.SemaphoreType.DMA((slots,)),
        ],
        compiler_params=PARAMS,
        name="spectrum",
    )(
        table_high.reshape(chips * 32, 256),
        table_low.reshape(chips * 32, 256),
        own_high,
        own_low,
        got,
    )

    rings = [[2 * chip + c for chip in range(chips)] for c in range(2)]
    summed = lax.psum_scatter(
        partial_sums.reshape(chips * planes * 32, wall_rows),
        "gx",
        scatter_dimension=0,
        axis_index_groups=rings,
        tiled=True,
    )

    lower_all, upper_all = spacing_bands(stretch_index)
    groups = planes // 4
    core_modes = lax.dynamic_slice_in_dim(mode_index.reshape(chips, 2, 16), core, 1, 1)
    weights = jax.ShapeDtypeStruct((groups, wall_rows * 8, 128), F32)
    first_row, last_row = pl.pallas_call(
        weights_kernel,
        out_shape=(weights, weights),
        in_specs=[SMEM, SMEM, SMEM, VMEM],
        out_specs=(VMEM, VMEM),
        compiler_params=PARAMS,
        name="weights",
    )(info, lower_all, upper_all, jnp.tile(core_modes.reshape(2, 128), (4, 1)))
    weight_spec = pl.BlockSpec((1, wall_rows * 8, 128), lambda i: (i, 0, 0))
    ends = pl.pallas_call(
        ends_kernel,
        out_shape=jax.ShapeDtypeStruct((2, 2, groups * 8, 128), F32),
        grid=(groups,),
        in_specs=[
            pl.BlockSpec((chips, 4, 32, wall_rows), lambda i: (0, i, 0, 0)),
            weight_spec,
            weight_spec,
        ],
        out_specs=pl.BlockSpec((2, 2, 8, 128), lambda i: (0, 0, i, 0)),
        compiler_params=PARAMS,
        name="ends",
    )(partial_sums, first_row, last_row)
    ends = ends.reshape(2, 2, planes, 2, 8, 16).transpose(3, 4, 0, 2, 1, 5)
    ends = ends.reshape(chips, 2, 8, 128)
    ends = jnp.take(ends, jnp.arange(chips) ^ (gx_index // 2), axis=0)
    distance = 1
    while distance < chips:
        pairs = ends.reshape(-1, 2, 2, 8, 128)
        route = [(i, i ^ (2 * distance)) for i in range(gx_count)]
        ends = pairs[:, 0] + lax.ppermute(pairs[:, 1], "gx", route)
        distance *= 2
    ends = ends.reshape(2, 8, 128)
    copies = jnp.broadcast_to(ends[None], (gy_count, 2, 8, 128))
    all_ends = lax.all_to_all(copies, "gy", split_axis=0, concat_axis=0, tiled=True)

    own_modes = lax.dynamic_slice_in_dim(mode_index, gx_index * 16, 16)
    own_modes = jnp.tile(own_modes, 8)[None, :]
    carry = pl.pallas_call(
        carry_kernel,
        out_shape=jax.ShapeDtypeStruct((6, gy_count, 8, 128), F32),
        in_specs=[SMEM, SMEM, VMEM],
        out_specs=VMEM,
        scratch_shapes=[pltpu.VMEM((4, gy_count, 8, 128), F32)],
        compiler_params=PARAMS,
        name="carry",
    )(lower_all, upper_all, own_modes)
    edges = pl.pallas_call(
        interface_kernel,
        out_shape=jax.ShapeDtypeStruct((2, 8, 128), F32),
        in_specs=[SMEM, VMEM, VMEM],
        out_specs=VMEM,
        scratch_shapes=[
            pltpu.VMEM((gy_count, 8, 128), F32),
            pltpu.VMEM((gy_count + 1, 8, 128), F32),
        ],
        compiler_params=PARAMS,
        name="interfaces",
    )(info, all_ends, carry)

    column = jax.ShapeDtypeStruct((wall_rows, 8, 128), F32)
    ratio, inverse, back = pl.pallas_call(
        own_factor_kernel,
        out_shape=(column,) * 3,
        in_specs=[SMEM, SMEM, SMEM, VMEM],
        out_specs=(VMEM,) * 3,
        compiler_params=PARAMS,
        name="own_factors",
    )(info, lower_all, upper_all, own_modes)

    summed, edges, ratio = lax.optimization_barrier((summed, edges, ratio))
    return pl.pallas_call(
        solve_kernel,
        out_shape=jax.ShapeDtypeStruct((2, planes, 16, wall_rows), F32),
        in_specs=[SMEM] * 3 + [VMEM] * 5,
        out_specs=VMEM,
        scratch_shapes=[pltpu.VMEM((planes * 32, wall_rows), F32)],
        compiler_params=PARAMS,
        name="solve",
    )(
        info,
        lower_all,
        upper_all,
        pltpu.with_memory_space_constraint(summed, pltpu.HBM),
        edges,
        ratio,
        inverse,
        back,
    )


def solution(mesh):
    in_specs = (P(None, "gx", "gy"), P(), P())
    out_specs = P(None, None, "gx", "gy")
    return jax.shard_map(local, mesh=mesh, in_specs=in_specs, out_specs=out_specs, check_vma=False)
```

```python
import functools
import math

import jax
import jax.numpy as jnp
from jax import lax
from jax.experimental import pallas as pl
from jax.experimental.pallas import tpu as pltpu
from jax.sharding import PartitionSpec as P

F32 = jnp.float32
BF16 = jnp.bfloat16
VMEM = pl.BlockSpec(memory_space=pltpu.VMEM)
SMEM = pl.BlockSpec(memory_space=pltpu.SMEM)
PARAMS = pltpu.CompilerParams(vmem_limit_bytes=48 * 1024 * 1024)


def spacing_bands(stretch_index):
    spacing = 0.25 * jnp.exp2(0.25 * stretch_index.astype(F32))
    faces = 0.5 * (spacing[:-1] + spacing[1:])
    zeros_one = jnp.zeros((1,), F32)
    lower_band = jnp.concatenate([zeros_one, 1.0 / (spacing[1:] * faces)])
    upper_band = jnp.concatenate([1.0 / (spacing[:-1] * faces), zeros_one])
    return (lower_band, upper_band)


def halves(values):
    high = values.astype(BF16)
    low = (values - high.astype(F32)).astype(BF16)
    return high, low


def wave(phase, length):
    quarter = length // 4
    phase = phase & (length - 1)
    turn = (phase + quarter // 2) // quarter
    angle = (phase - turn * quarter).astype(F32) * (2.0 * math.pi / length)
    square = angle * angle
    sine = angle * (
        1.0
        + square
        * (-1.0 / 6 + square * (1.0 / 120 + square * (-1.0 / 5040 + square * (1.0 / 362880))))
    )
    cosine = 1.0 + square * (
        -0.5 + square * (1.0 / 24 + square * (-1.0 / 720 + square * (1.0 / 40320)))
    )
    odd = (turn & 1) == 1
    real = jnp.where(odd, sine, cosine)
    imag = jnp.where(odd, cosine, sine)
    real = jnp.where(((turn + 1) & 2) == 2, -real, real)
    imag = jnp.where((turn & 2) == 2, -imag, imag)
    return real, imag


def table_kernel(
    length, info_ref, modes_ref, own_ref, table_ref, own_high_ref, own_low_ref, own, sems
):
    core, index = info_ref[0], info_ref[2]
    steps = sems.shape[0]
    some = own_ref.shape[0] // steps
    groups = [pl.ds(some * g, some) for g in range(steps)]
    loads = [
        pltpu.make_async_copy(own_ref.at[groups[g]], own.at[groups[g]], sems.at[g])
        for g in range(steps)
    ]
    for load in loads:
        load.start()
    chips = table_ref.shape[0]
    mode_column = jnp.concatenate([modes_ref[2 * chip + core] for chip in range(chips)], 0)
    for side in range(2):
        start = 128 * (index ^ side)
        place = start + lax.broadcasted_iota(jnp.int32, (1, 128), 1)
        real, imag = wave(mode_column * place, length)
        scale = 1.0 / math.sqrt(length)
        for part, values in enumerate((real * scale, imag * -scale)):
            high, low = halves(values)
            for third, half in enumerate((high, high, low)):
                columns = pl.ds(third * 256 + side * 128, 128)
                table_ref[:, part, :, columns] = half.reshape(-1, 16, 128)
    for g in range(steps):
        loads[g].wait()
        own_high_ref[groups[g]], own_low_ref[groups[g]] = halves(own[groups[g]])


def spectrum_kernel(plan, table_ref, own_high_ref, own_low_ref, got_ref, out_ref, sums, out_sems):
    slots, chips = sums.shape[:2]
    steps = len(plan)
    bounds = [sum(plan[:g]) for g in range(steps)]
    stores = [
        pltpu.make_async_copy(
            sums.at[g % slots, :, pl.ds(0, plan[g])],
            out_ref.at[:, pl.ds(bounds[g], plan[g])],
            out_sems.at[g % slots],
        )
        for g in range(steps)
    ]

    def beside(ref, plane):
        return jnp.concatenate([ref[plane], ref[plane + 1]], 1)

    for g in range(steps):
        if g >= slots:
            stores[g - slots].wait()
        for pair in range(0, plan[g], 2):
            plane = bounds[g] + pair
            got_high, got_low = halves(beside(got_ref, plane))
            field_high = jnp.concatenate([beside(own_high_ref, plane), got_high], 0)
            field_low = jnp.concatenate([beside(own_low_ref, plane), got_low], 0)
            fields = jnp.concatenate([field_high, field_low, field_high], 0)
            step = 8
            for first in range(0, chips, step):
                rows = pl.ds(first * 32, step * 32)
                total = jnp.dot(table_ref[rows, :], fields, preferred_element_type=F32)
                for k in range(2):
                    piece = total[:, k * 128 : (k + 1) * 128].reshape(step, 32, 128)
                    sums[g % slots, pl.ds(first, step), pair + k] = piece
        stores[g].start()
    for g in range(max(0, steps - slots), steps):
        stores[g].wait()


def shift_of(plane, modes):
    span_wave = 0.04 * (plane.astype(F32) + 1.0)
    stream_wave = modes.astype(F32) * (2.0 * math.pi / 4096)
    return span_wave * span_wave + stream_wave * stream_wave


def carry_kernel(low_ref, up_ref, modes_ref, carry_ref, corner):
    rows = 128
    blocks = carry_ref.shape[1]
    sublane = lax.broadcasted_iota(jnp.int32, (8, 128), 0)
    lane = lax.broadcasted_iota(jnp.int32, (8, 128), 1)
    shift = shift_of(4 * sublane + lane // 32, modes_ref[...])

    group = 8
    for first in range(0, blocks, group):
        state = []
        for b in range(first, first + group):
            low, up = low_ref[b * rows], up_ref[b * rows]
            inverse = 1.0 / (low + up + shift)
            state.append((inverse, jnp.ones_like(shift), up * inverse, inverse))

        def forward(j, state):
            later = []
            for k in range(group):
                at = (first + k) * rows + j
                low, up, before = low_ref[at], up_ref[at], up_ref[at - 1]
                inverse, chain, product, corner_sum = state[k]
                ratio = low * inverse
                inverse = 1.0 / (low + up + shift - ratio * before)
                chain = chain * ratio
                corner_sum = corner_sum + product * (chain * inverse)
                later.append((inverse, chain, product * (up * inverse), corner_sum))
            return tuple(later)

        state = lax.fori_loop(1, rows, forward, tuple(state))
        for k in range(group):
            b = first + k
            inverse, chain, product, corner_sum = state[k]
            low, up = low_ref[b * rows], up_ref[b * rows + rows - 1]
            corner[0, b] = low * corner_sum
            corner[1, b] = low * (chain * inverse)
            corner[2, b] = product
            corner[3, b] = up * inverse

    reach = jnp.zeros_like(shift)
    for b in range(blocks):
        left_first, left_last = corner[0, b], corner[1, b]
        right_first, right_last = corner[2, b], corner[3, b]
        gain = 1.0 / (1.0 - left_first * reach)
        carry_ref[0, b] = left_last * gain
        carry_ref[1, b] = left_last * reach * gain
        carry_ref[2, b] = gain
        carry_ref[3, b] = gain * left_first
        carry_ref[4, b] = gain * right_first
        carry_ref[5, b] = reach
        reach = right_last + left_last * reach * gain * right_first


def weights_kernel(info_ref, low_ref, up_ref, modes_ref, first_ref, last_ref):
    rows = 128
    groups = first_ref.shape[0]
    start = info_ref[1] * rows
    end = start + rows - 1
    sublane = lax.broadcasted_iota(jnp.int32, (8, 128), 0)
    shifts = [shift_of(4 * w + sublane // 2, modes_ref[...]) for w in range(groups)]

    state = []
    for w in range(groups):
        down = 1.0 / (low_ref[start] + up_ref[start] + shifts[w])
        rising = 1.0 / (low_ref[end] + up_ref[end] + shifts[w])
        last_ref[w, pl.ds(0, 8), :] = down
        first_ref[w, pl.ds(8 * (rows - 1), 8), :] = rising
        state += [down, rising]

    def eliminate(i, state):
        j, k = start + i, end - i
        later = []
        for w in range(groups):
            down, rising = state[2 * w], state[2 * w + 1]
            down = 1.0 / (low_ref[j] + up_ref[j] + shifts[w] - (low_ref[j] * down) * up_ref[j - 1])
            last_ref[w, pl.ds(pl.multiple_of(8 * i, 8), 8), :] = down
            rising = 1.0 / (
                low_ref[k] + up_ref[k] + shifts[w] - (up_ref[k] * rising) * low_ref[k + 1]
            )
            first_ref[w, pl.ds(pl.multiple_of(8 * (rows - 1 - i), 8), 8), :] = rising
            later += [down, rising]
        return tuple(later)

    state = lax.fori_loop(1, rows, eliminate, tuple(state))

    def spread(i, state):
        j = rows - 1 - i
        later = []
        for w in range(groups):
            last, first = state[2 * w], state[2 * w + 1]
            at = pl.ds(pl.multiple_of(8 * j, 8), 8)
            last = last * (low_ref[start + j + 1] * last_ref[w, at, :])
            last_ref[w, at, :] = last
            at = pl.ds(pl.multiple_of(8 * i, 8), 8)
            first = first * (up_ref[start + i - 1] * first_ref[w, at, :])
            first_ref[w, at, :] = first
            later += [last, first]
        return tuple(later)

    lax.fori_loop(1, rows, spread, state)


def ends_kernel(sums_ref, first_ref, last_ref, ends_ref):
    for row in range(8):
        plane, half = row // 2, row % 2
        at = pl.ds(row, 128, stride=8)
        first, last = first_ref[0, at, :], last_ref[0, at, :]
        for part in range(2):
            values = sums_ref[pl.ds(8 * half, 8), plane, pl.ds(16 * part, 16), :]
            values = values.reshape(128, 128).T
            ends_ref[0, part, pl.ds(row, 1), :] = jnp.sum(values * first, 0, keepdims=True)
            ends_ref[1, part, pl.ds(row, 1), :] = jnp.sum(values * last, 0, keepdims=True)


def interface_kernel(info_ref, ends_ref, carry_ref, edge_ref, sums, firsts):
    block = info_ref[1]
    blocks = ends_ref.shape[0]
    before = jnp.zeros((8, 128), F32)
    for b in range(blocks):
        sums[b] = before
        before = ends_ref[b, 1] + carry_ref[1, b] * ends_ref[b, 0] + carry_ref[0, b] * before
    after = jnp.zeros((8, 128), F32)
    for b in reversed(range(blocks)):
        firsts[b + 1] = after
        base = carry_ref[2, b] * ends_ref[b, 0] + carry_ref[3, b] * sums[b]
        after = base + carry_ref[4, b] * after
    firsts[0] = after
    edge_ref[0] = sums[block] + carry_ref[5, block] * firsts[block]
    edge_ref[1] = firsts[block + 1]


def own_factor_kernel(info_ref, low_ref, up_ref, modes_ref, ratio_ref, inverse_ref, back_ref):
    rows = 128
    half = rows // 2
    sublane = lax.broadcasted_iota(jnp.int32, (8, 128), 0)
    lane = lax.broadcasted_iota(jnp.int32, (8, 128), 1)
    shift = shift_of(4 * sublane + lane // 32, modes_ref[...])
    start = info_ref[1] * rows
    end = start + rows - 1

    def pivot(at):
        return low_ref[at] + up_ref[at] + shift

    down = 1.0 / pivot(start)
    rising = 1.0 / pivot(end)
    ratio_ref[0] = jnp.zeros_like(shift)
    ratio_ref[rows - 1] = jnp.zeros_like(shift)
    inverse_ref[0] = down
    inverse_ref[rows - 1] = rising
    back_ref[0] = up_ref[start] * down
    back_ref[rows - 1] = low_ref[end] * rising

    def eliminate(i, state):
        down, rising = state
        j, k = start + i, end - i
        ratio = low_ref[j] * down
        down = 1.0 / (pivot(j) - ratio * up_ref[j - 1])
        ratio_ref[i] = ratio
        inverse_ref[i] = down
        back_ref[i] = up_ref[j] * down
        ratio = up_ref[k] * rising
        rising = 1.0 / (pivot(k) - ratio * low_ref[k + 1])
        ratio_ref[rows - 1 - i] = ratio
        inverse_ref[rows - 1 - i] = rising
        back_ref[rows - 1 - i] = low_ref[k] * rising
        return (down, rising)

    down, rising = lax.fori_loop(1, half, eliminate, (down, rising))
    across = 1.0 / (1.0 - back_ref[half - 1] * back_ref[half])
    inverse_ref[half - 1] = down * across
    inverse_ref[half] = rising * across


def solve_kernel(
    info_ref,
    low_ref,
    up_ref,
    sums_ref,
    edge_ref,
    ratio_ref,
    inverse_ref,
    back_ref,
    out_ref,
    work,
):
    rows = 128
    half = rows // 2
    start = info_ref[1] * rows
    for k in range(8):
        work[pl.ds(k, rows, stride=8), :] = sums_ref[pl.ds(rows * k, rows), :].T

    def row(j):
        return pl.ds(pl.multiple_of(j * 8, 8), 8)

    upper = work[row(0), :] + low_ref[start] * edge_ref[0]
    lower = work[row(rows - 1), :] + up_ref[start + rows - 1] * edge_ref[1]
    work[row(0), :] = upper
    work[row(rows - 1), :] = lower

    def inwards(j, state):
        upper, lower = state
        k = rows - 1 - j
        upper = work[row(j), :] + ratio_ref[j] * upper
        work[row(j), :] = upper
        lower = work[row(k), :] + ratio_ref[k] * lower
        work[row(k), :] = lower
        return (upper, lower)

    upper, lower = lax.fori_loop(1, half, inwards, (upper, lower), unroll=63)

    first = upper * inverse_ref[half - 1]
    second = lower * inverse_ref[half]
    upper = first + back_ref[half - 1] * second
    lower = second + back_ref[half] * first
    work[row(half - 1), :] = upper
    work[row(half), :] = lower

    def outwards(i, state):
        upper, lower = state
        j = half - 1 - i
        k = half + i
        upper = work[row(j), :] * inverse_ref[j] + back_ref[j] * upper
        work[row(j), :] = upper
        lower = work[row(k), :] * inverse_ref[k] + back_ref[k] * lower
        work[row(k), :] = lower
        return (upper, lower)

    lax.fori_loop(1, half, outwards, (upper, lower), unroll=63)
    for k in range(8):
        piece = work[pl.ds(k, rows, stride=8), :].T
        for z in range(4):
            for part in range(2):
                at = z * 32 + part * 16
                out_ref[part, 4 * k + z] = piece[at : at + 16]


def local(source, stretch_index, mode_index):
    gx_count = lax.axis_size("gx")
    gy_count = lax.axis_size("gy")
    planes, stream_rows, wall_rows = source.shape
    length = stream_rows * gx_count
    gx_index = lax.axis_index("gx")
    gy_index = lax.axis_index("gy")
    core = gx_index % 2
    chips = gx_count // 2
    info = jnp.stack([core, gy_index, gx_index]).astype(jnp.int32)

    got = lax.ppermute(source, "gx", [(i, i ^ 1) for i in range(gx_count)])
    hbm = pl.BlockSpec(memory_space=pltpu.HBM)
    source = pltpu.with_memory_space_constraint(source, pltpu.HBM)
    table_shape = jax.ShapeDtypeStruct((chips, 2, 16, 768), BF16)
    own_shape = jax.ShapeDtypeStruct(source.shape, BF16)
    table, own_high, own_low = pl.pallas_call(
        functools.partial(table_kernel, length),
        out_shape=(table_shape, own_shape, own_shape),
        in_specs=[SMEM, VMEM, hbm],
        out_specs=(VMEM,) * 3,
        scratch_shapes=[pltpu.VMEM(source.shape, F32), pltpu.SemaphoreType.DMA((4,))],
        compiler_params=PARAMS,
        name="tables",
    )(info, mode_index.reshape(gx_count, 16, 1), source)

    plan = (4, 8, 8, 8, 4)
    slots = 3
    partial_sums = pl.pallas_call(
        functools.partial(spectrum_kernel, plan),
        out_shape=jax.ShapeDtypeStruct((chips, planes, 32, wall_rows), F32),
        in_specs=[VMEM] * 4,
        out_specs=hbm,
        scratch_shapes=[
            pltpu.VMEM((slots, chips, max(plan), 32, wall_rows), F32),
            pltpu.SemaphoreType.DMA((slots,)),
        ],
        compiler_params=PARAMS,
        name="spectrum",
    )(
        table.reshape(chips * 32, 768),
        own_high,
        own_low,
        got,
    )

    rings = [[2 * chip + c for chip in range(chips)] for c in range(2)]
    summed = lax.psum_scatter(
        partial_sums.reshape(chips * planes * 32, wall_rows),
        "gx",
        scatter_dimension=0,
        axis_index_groups=rings,
        tiled=True,
    )

    lower_all, upper_all = spacing_bands(stretch_index)
    groups = planes // 4
    core_modes = lax.dynamic_slice_in_dim(mode_index.reshape(chips, 2, 16), core, 1, 1)
    weights = jax.ShapeDtypeStruct((groups, wall_rows * 8, 128), F32)
    first_row, last_row = pl.pallas_call(
        weights_kernel,
        out_shape=(weights, weights),
        in_specs=[SMEM, SMEM, SMEM, VMEM],
        out_specs=(VMEM, VMEM),
        compiler_params=PARAMS,
        name="weights",
    )(info, lower_all, upper_all, jnp.tile(core_modes.reshape(2, 128), (4, 1)))
    weight_spec = pl.BlockSpec((1, wall_rows * 8, 128), lambda i: (i, 0, 0))
    ends = pl.pallas_call(
        ends_kernel,
        out_shape=jax.ShapeDtypeStruct((2, 2, groups * 8, 128), F32),
        grid=(groups,),
        in_specs=[
            pl.BlockSpec((chips, 4, 32, wall_rows), lambda i: (0, i, 0, 0)),
            weight_spec,
            weight_spec,
        ],
        out_specs=pl.BlockSpec((2, 2, 8, 128), lambda i: (0, 0, i, 0)),
        compiler_params=PARAMS,
        name="ends",
    )(partial_sums, first_row, last_row)
    ends = ends.reshape(2, 2, planes, 2, 8, 16).transpose(3, 4, 0, 2, 1, 5)
    ends = ends.reshape(chips, 2, 8, 128)
    ends = jnp.take(ends, jnp.arange(chips) ^ (gx_index // 2), axis=0)
    distance = 1
    while distance < chips:
        pairs = ends.reshape(-1, 2, 2, 8, 128)
        route = [(i, i ^ (2 * distance)) for i in range(gx_count)]
        ends = pairs[:, 0] + lax.ppermute(pairs[:, 1], "gx", route)
        distance *= 2
    ends = ends.reshape(2, 8, 128)
    copies = jnp.broadcast_to(ends[None], (gy_count, 2, 8, 128))
    all_ends = lax.all_to_all(copies, "gy", split_axis=0, concat_axis=0, tiled=True)

    own_modes = lax.dynamic_slice_in_dim(mode_index, gx_index * 16, 16)
    own_modes = jnp.tile(own_modes, 8)[None, :]
    carry = pl.pallas_call(
        carry_kernel,
        out_shape=jax.ShapeDtypeStruct((6, gy_count, 8, 128), F32),
        in_specs=[SMEM, SMEM, VMEM],
        out_specs=VMEM,
        scratch_shapes=[pltpu.VMEM((4, gy_count, 8, 128), F32)],
        compiler_params=PARAMS,
        name="carry",
    )(lower_all, upper_all, own_modes)
    edges = pl.pallas_call(
        interface_kernel,
        out_shape=jax.ShapeDtypeStruct((2, 8, 128), F32),
        in_specs=[SMEM, VMEM, VMEM],
        out_specs=VMEM,
        scratch_shapes=[
            pltpu.VMEM((gy_count, 8, 128), F32),
            pltpu.VMEM((gy_count + 1, 8, 128), F32),
        ],
        compiler_params=PARAMS,
        name="interfaces",
    )(info, all_ends, carry)

    column = jax.ShapeDtypeStruct((wall_rows, 8, 128), F32)
    ratio, inverse, back = pl.pallas_call(
        own_factor_kernel,
        out_shape=(column,) * 3,
        in_specs=[SMEM, SMEM, SMEM, VMEM],
        out_specs=(VMEM,) * 3,
        compiler_params=PARAMS,
        name="own_factors",
    )(info, lower_all, upper_all, own_modes)

    summed, edges, ratio = lax.optimization_barrier((summed, edges, ratio))
    return pl.pallas_call(
        solve_kernel,
        out_shape=jax.ShapeDtypeStruct((2, planes, 16, wall_rows), F32),
        in_specs=[SMEM] * 3 + [VMEM] * 5,
        out_specs=VMEM,
        scratch_shapes=[pltpu.VMEM((planes * 32, wall_rows), F32)],
        compiler_params=PARAMS,
        name="solve",
    )(
        info,
        lower_all,
        upper_all,
        pltpu.with_memory_space_constraint(summed, pltpu.HBM),
        edges,
        ratio,
        inverse,
        back,
    )


def solution(mesh):
    in_specs = (P(None, "gx", "gy"), P(), P())
    out_specs = P(None, None, "gx", "gy")
    return jax.shard_map(local, mesh=mesh, in_specs=in_specs, out_specs=out_specs, check_vma=False)
```

```python
import functools
import math

import jax
import jax.numpy as jnp
from jax import lax
from jax.experimental import pallas as pl
from jax.experimental.pallas import tpu as pltpu
from jax.sharding import PartitionSpec as P

F32 = jnp.float32
BF16 = jnp.bfloat16
VMEM = pl.BlockSpec(memory_space=pltpu.VMEM)
SMEM = pl.BlockSpec(memory_space=pltpu.SMEM)
PARAMS = pltpu.CompilerParams(vmem_limit_bytes=48 * 1024 * 1024)


def spacing_bands(stretch_index):
    spacing = 0.25 * jnp.exp2(0.25 * stretch_index.astype(F32))
    faces = 0.5 * (spacing[:-1] + spacing[1:])
    zeros_one = jnp.zeros((1,), F32)
    lower_band = jnp.concatenate([zeros_one, 1.0 / (spacing[1:] * faces)])
    upper_band = jnp.concatenate([1.0 / (spacing[:-1] * faces), zeros_one])
    return (lower_band, upper_band)


def halves(values):
    high = values.astype(BF16)
    low = (values - high.astype(F32)).astype(BF16)
    return high, low


def wave(phase, length):
    quarter = length // 4
    phase = phase & (length - 1)
    turn = (phase + quarter // 2) // quarter
    angle = (phase - turn * quarter).astype(F32) * (2.0 * math.pi / length)
    square = angle * angle
    sine = angle * (
        1.0
        + square
        * (-1.0 / 6 + square * (1.0 / 120 + square * (-1.0 / 5040 + square * (1.0 / 362880))))
    )
    cosine = 1.0 + square * (
        -0.5 + square * (1.0 / 24 + square * (-1.0 / 720 + square * (1.0 / 40320)))
    )
    odd = (turn & 1) == 1
    real = jnp.where(odd, sine, cosine)
    imag = jnp.where(odd, cosine, sine)
    real = jnp.where(((turn + 1) & 2) == 2, -real, real)
    imag = jnp.where((turn & 2) == 2, -imag, imag)
    return real, imag


def table_kernel(
    length, info_ref, modes_ref, own_ref, high_ref, low_ref, own_high_ref, own_low_ref, own, sems
):
    core, index = info_ref[0], info_ref[2]
    steps = sems.shape[0]
    some = own_ref.shape[0] // steps
    groups = [pl.ds(some * g, some) for g in range(steps)]
    loads = [
        pltpu.make_async_copy(own_ref.at[groups[g]], own.at[groups[g]], sems.at[g])
        for g in range(steps)
    ]
    for load in loads:
        load.start()
    chips = high_ref.shape[0]
    mode_column = jnp.concatenate([modes_ref[2 * chip + core] for chip in range(chips)], 0)
    for side in range(2):
        start = 128 * (index ^ side)
        place = start + lax.broadcasted_iota(jnp.int32, (1, 128), 1)
        real, imag = wave(mode_column * place, length)
        scale = 1.0 / math.sqrt(length)
        columns = pl.ds(side * 128, 128)
        for part, values in enumerate((real * scale, imag * -scale)):
            high, low = halves(values)
            high_ref[:, part, :, columns] = high.reshape(-1, 16, 128)
            low_ref[:, part, :, columns] = low.reshape(-1, 16, 128)
    for g in range(steps):
        loads[g].wait()
        own_high_ref[groups[g]], own_low_ref[groups[g]] = halves(own[groups[g]])


def spectrum_kernel(
    high_ref, low_ref, own_high_ref, own_low_ref, got_ref, out_ref, sums, out_sems
):
    slots, chips, some = sums.shape[:3]
    steps = got_ref.shape[0] // some
    stores = [
        pltpu.make_async_copy(
            sums.at[g % slots], out_ref.at[:, pl.ds(some * g, some)], out_sems.at[g % slots]
        )
        for g in range(steps)
    ]

    def beside(ref, plane):
        return jnp.concatenate([ref[plane], ref[plane + 1]], 1)

    for g in range(steps):
        if g >= slots:
            stores[g - slots].wait()
        for pair in range(0, some, 2):
            plane = some * g + pair
            got_high, got_low = halves(beside(got_ref, plane))
            field_high = jnp.concatenate([beside(own_high_ref, plane), got_high], 0)
            field_low = jnp.concatenate([beside(own_low_ref, plane), got_low], 0)
            step = 8
            for first in range(0, chips, step):
                rows = pl.ds(first * 32, step * 32)
                high = high_ref[rows, :]
                total = jnp.dot(high, field_high, preferred_element_type=F32)
                total += jnp.dot(high, field_low, preferred_element_type=F32)
                total += jnp.dot(low_ref[rows, :], field_high, preferred_element_type=F32)
                for k in range(2):
                    piece = total[:, k * 128 : (k + 1) * 128].reshape(step, 32, 128)
                    sums[g % slots, pl.ds(first, step), pair + k] = piece
        stores[g].start()
    for g in range(max(0, steps - slots), steps):
        stores[g].wait()


def shift_of(plane, modes):
    span_wave = 0.04 * (plane.astype(F32) + 1.0)
    stream_wave = modes.astype(F32) * (2.0 * math.pi / 4096)
    return span_wave * span_wave + stream_wave * stream_wave


def carry_kernel(low_ref, up_ref, modes_ref, carry_ref, corner):
    rows = 128
    blocks = carry_ref.shape[1]
    sublane = lax.broadcasted_iota(jnp.int32, (8, 128), 0)
    lane = lax.broadcasted_iota(jnp.int32, (8, 128), 1)
    shift = shift_of(4 * sublane + lane // 32, modes_ref[...])

    group = 8
    for first in range(0, blocks, group):
        state = []
        for b in range(first, first + group):
            low, up = low_ref[b * rows], up_ref[b * rows]
            inverse = 1.0 / (low + up + shift)
            state.append((inverse, jnp.ones_like(shift), up * inverse, inverse))

        def forward(j, state):
            later = []
            for k in range(group):
                at = (first + k) * rows + j
                low, up, before = low_ref[at], up_ref[at], up_ref[at - 1]
                inverse, chain, product, corner_sum = state[k]
                ratio = low * inverse
                inverse = 1.0 / (low + up + shift - ratio * before)
                chain = chain * ratio
                corner_sum = corner_sum + product * (chain * inverse)
                later.append((inverse, chain, product * (up * inverse), corner_sum))
            return tuple(later)

        state = lax.fori_loop(1, rows, forward, tuple(state))
        for k in range(group):
            b = first + k
            inverse, chain, product, corner_sum = state[k]
            low, up = low_ref[b * rows], up_ref[b * rows + rows - 1]
            corner[0, b] = low * corner_sum
            corner[1, b] = low * (chain * inverse)
            corner[2, b] = product
            corner[3, b] = up * inverse

    reach = jnp.zeros_like(shift)
    for b in range(blocks):
        left_first, left_last = corner[0, b], corner[1, b]
        right_first, right_last = corner[2, b], corner[3, b]
        gain = 1.0 / (1.0 - left_first * reach)
        carry_ref[0, b] = left_last * gain
        carry_ref[1, b] = left_last * reach * gain
        carry_ref[2, b] = gain
        carry_ref[3, b] = gain * left_first
        carry_ref[4, b] = gain * right_first
        carry_ref[5, b] = reach
        reach = right_last + left_last * reach * gain * right_first


def weights_kernel(info_ref, low_ref, up_ref, modes_ref, first_ref, last_ref):
    rows = 128
    groups = first_ref.shape[0]
    start = info_ref[1] * rows
    end = start + rows - 1
    sublane = lax.broadcasted_iota(jnp.int32, (8, 128), 0)
    shifts = [shift_of(4 * w + sublane // 2, modes_ref[...]) for w in range(groups)]

    state = []
    for w in range(groups):
        down = 1.0 / (low_ref[start] + up_ref[start] + shifts[w])
        rising = 1.0 / (low_ref[end] + up_ref[end] + shifts[w])
        last_ref[w, pl.ds(0, 8), :] = down
        first_ref[w, pl.ds(8 * (rows - 1), 8), :] = rising
        state += [down, rising]

    def eliminate(i, state):
        j, k = start + i, end - i
        later = []
        for w in range(groups):
            down, rising = state[2 * w], state[2 * w + 1]
            down = 1.0 / (low_ref[j] + up_ref[j] + shifts[w] - (low_ref[j] * down) * up_ref[j - 1])
            last_ref[w, pl.ds(pl.multiple_of(8 * i, 8), 8), :] = down
            rising = 1.0 / (
                low_ref[k] + up_ref[k] + shifts[w] - (up_ref[k] * rising) * low_ref[k + 1]
            )
            first_ref[w, pl.ds(pl.multiple_of(8 * (rows - 1 - i), 8), 8), :] = rising
            later += [down, rising]
        return tuple(later)

    state = lax.fori_loop(1, rows, eliminate, tuple(state))

    def spread(i, state):
        j = rows - 1 - i
        later = []
        for w in range(groups):
            last, first = state[2 * w], state[2 * w + 1]
            at = pl.ds(pl.multiple_of(8 * j, 8), 8)
            last = last * (low_ref[start + j + 1] * last_ref[w, at, :])
            last_ref[w, at, :] = last
            at = pl.ds(pl.multiple_of(8 * i, 8), 8)
            first = first * (up_ref[start + i - 1] * first_ref[w, at, :])
            first_ref[w, at, :] = first
            later += [last, first]
        return tuple(later)

    lax.fori_loop(1, rows, spread, state)


def ends_kernel(sums_ref, first_ref, last_ref, ends_ref):
    for row in range(8):
        plane, half = row // 2, row % 2
        at = pl.ds(row, 128, stride=8)
        first, last = first_ref[0, at, :], last_ref[0, at, :]
        for part in range(2):
            values = sums_ref[pl.ds(8 * half, 8), plane, pl.ds(16 * part, 16), :]
            values = values.reshape(128, 128).T
            ends_ref[0, part, pl.ds(row, 1), :] = jnp.sum(values * first, 0, keepdims=True)
            ends_ref[1, part, pl.ds(row, 1), :] = jnp.sum(values * last, 0, keepdims=True)


def interface_kernel(info_ref, low_ref, up_ref, ends_ref, carry_ref, edge_ref, sums, firsts):
    block = info_ref[1]
    blocks = ends_ref.shape[0]
    before = jnp.zeros((8, 128), F32)
    for b in range(blocks):
        sums[b] = before
        before = ends_ref[b, 1] + carry_ref[1, b] * ends_ref[b, 0] + carry_ref[0, b] * before
    after = jnp.zeros((8, 128), F32)
    for b in reversed(range(blocks)):
        firsts[b + 1] = after
        base = carry_ref[2, b] * ends_ref[b, 0] + carry_ref[3, b] * sums[b]
        after = base + carry_ref[4, b] * after
    firsts[0] = after
    below = sums[block] + carry_ref[5, block] * firsts[block]
    edge_ref[0] = low_ref[128 * block] * below
    edge_ref[1] = up_ref[128 * block + 127] * firsts[block + 1]


def own_factor_kernel(info_ref, low_ref, up_ref, modes_ref, ratio_ref, inverse_ref, back_ref):
    rows = 128
    half = rows // 2
    sublane = lax.broadcasted_iota(jnp.int32, (8, 128), 0)
    lane = lax.broadcasted_iota(jnp.int32, (8, 128), 1)
    shift = shift_of(4 * sublane + lane // 32, modes_ref[...])
    start = info_ref[1] * rows
    end = start + rows - 1

    def pivot(at):
        return low_ref[at] + up_ref[at] + shift

    down = 1.0 / pivot(start)
    rising = 1.0 / pivot(end)
    ratio_ref[0] = jnp.zeros_like(shift)
    ratio_ref[rows - 1] = jnp.zeros_like(shift)
    inverse_ref[0] = down
    inverse_ref[rows - 1] = rising
    back_ref[0] = up_ref[start] * down
    back_ref[rows - 1] = low_ref[end] * rising

    def eliminate(i, state):
        down, rising = state
        j, k = start + i, end - i
        ratio = low_ref[j] * down
        down = 1.0 / (pivot(j) - ratio * up_ref[j - 1])
        ratio_ref[i] = ratio
        inverse_ref[i] = down
        back_ref[i] = up_ref[j] * down
        ratio = up_ref[k] * rising
        rising = 1.0 / (pivot(k) - ratio * low_ref[k + 1])
        ratio_ref[rows - 1 - i] = ratio
        inverse_ref[rows - 1 - i] = rising
        back_ref[rows - 1 - i] = low_ref[k] * rising
        return (down, rising)

    down, rising = lax.fori_loop(1, half, eliminate, (down, rising))
    across = 1.0 / (1.0 - back_ref[half - 1] * back_ref[half])
    inverse_ref[half - 1] = down * across
    inverse_ref[half] = rising * across


def solve_kernel(
    sums_ref,
    edge_ref,
    ratio_ref,
    inverse_ref,
    back_ref,
    out_ref,
    work,
):
    rows = 128
    half = rows // 2
    for k in range(8):
        work[pl.ds(k, rows, stride=8), :] = sums_ref[pl.ds(rows * k, rows), :].T

    def row(j):
        return pl.ds(pl.multiple_of(j * 8, 8), 8)

    upper = work[row(0), :] + edge_ref[0]
    lower = work[row(rows - 1), :] + edge_ref[1]
    work[row(0), :] = upper
    work[row(rows - 1), :] = lower

    def inwards(j, state):
        upper, lower = state
        k = rows - 1 - j
        upper = work[row(j), :] + ratio_ref[j] * upper
        work[row(j), :] = upper
        lower = work[row(k), :] + ratio_ref[k] * lower
        work[row(k), :] = lower
        return (upper, lower)

    upper, lower = lax.fori_loop(1, half, inwards, (upper, lower), unroll=63)

    first = upper * inverse_ref[half - 1]
    second = lower * inverse_ref[half]
    upper = first + back_ref[half - 1] * second
    lower = second + back_ref[half] * first
    work[row(half - 1), :] = upper
    work[row(half), :] = lower

    def outwards(i, state):
        upper, lower = state
        j = half - 1 - i
        k = half + i
        upper = work[row(j), :] * inverse_ref[j] + back_ref[j] * upper
        work[row(j), :] = upper
        lower = work[row(k), :] * inverse_ref[k] + back_ref[k] * lower
        work[row(k), :] = lower
        return (upper, lower)

    lax.fori_loop(1, half, outwards, (upper, lower), unroll=63)
    for k in range(8):
        piece = work[pl.ds(k, rows, stride=8), :].T
        for z in range(4):
            for part in range(2):
                at = z * 32 + part * 16
                out_ref[part, 4 * k + z] = piece[at : at + 16]


def local(source, stretch_index, mode_index):
    gx_count = lax.axis_size("gx")
    gy_count = lax.axis_size("gy")
    planes, stream_rows, wall_rows = source.shape
    length = stream_rows * gx_count
    gx_index = lax.axis_index("gx")
    gy_index = lax.axis_index("gy")
    core = gx_index % 2
    chips = gx_count // 2
    info = jnp.stack([core, gy_index, gx_index]).astype(jnp.int32)

    got = lax.ppermute(source, "gx", [(i, i ^ 1) for i in range(gx_count)])
    hbm = pl.BlockSpec(memory_space=pltpu.HBM)
    source = pltpu.with_memory_space_constraint(source, pltpu.HBM)
    table_shape = jax.ShapeDtypeStruct((chips, 2, 16, 256), BF16)
    own_shape = jax.ShapeDtypeStruct(source.shape, BF16)
    table_high, table_low, own_high, own_low = pl.pallas_call(
        functools.partial(table_kernel, length),
        out_shape=(table_shape, table_shape, own_shape, own_shape),
        in_specs=[SMEM, VMEM, hbm],
        out_specs=(VMEM,) * 4,
        scratch_shapes=[pltpu.VMEM(source.shape, F32), pltpu.SemaphoreType.DMA((4,))],
        compiler_params=PARAMS,
        name="tables",
    )(info, mode_index.reshape(gx_count, 16, 1), source)

    some = 8
    slots = 3
    partial_sums = pl.pallas_call(
        spectrum_kernel,
        out_shape=jax.ShapeDtypeStruct((chips, planes, 32, wall_rows), F32),
        in_specs=[VMEM] * 5,
        out_specs=hbm,
        scratch_shapes=[
            pltpu.VMEM((slots, chips, some, 32, wall_rows), F32),
            pltpu.SemaphoreType.DMA((slots,)),
        ],
        compiler_params=PARAMS,
        name="spectrum",
    )(
        table_high.reshape(chips * 32, 256),
        table_low.reshape(chips * 32, 256),
        own_high,
        own_low,
        got,
    )

    rings = [[2 * chip + c for chip in range(chips)] for c in range(2)]
    summed = lax.psum_scatter(
        partial_sums.reshape(chips * planes * 32, wall_rows),
        "gx",
        scatter_dimension=0,
        axis_index_groups=rings,
        tiled=True,
    )

    lower_all, upper_all = spacing_bands(stretch_index)
    groups = planes // 4
    core_modes = lax.dynamic_slice_in_dim(mode_index.reshape(chips, 2, 16), core, 1, 1)
    weights = jax.ShapeDtypeStruct((groups, wall_rows * 8, 128), F32)
    first_row, last_row = pl.pallas_call(
        weights_kernel,
        out_shape=(weights, weights),
        in_specs=[SMEM, SMEM, SMEM, VMEM],
        out_specs=(VMEM, VMEM),
        compiler_params=PARAMS,
        name="weights",
    )(info, lower_all, upper_all, jnp.tile(core_modes.reshape(2, 128), (4, 1)))
    weight_spec = pl.BlockSpec((1, wall_rows * 8, 128), lambda i: (i, 0, 0))
    ends = pl.pallas_call(
        ends_kernel,
        out_shape=jax.ShapeDtypeStruct((2, 2, groups * 8, 128), F32),
        grid=(groups,),
        in_specs=[
            pl.BlockSpec((chips, 4, 32, wall_rows), lambda i: (0, i, 0, 0)),
            weight_spec,
            weight_spec,
        ],
        out_specs=pl.BlockSpec((2, 2, 8, 128), lambda i: (0, 0, i, 0)),
        compiler_params=PARAMS,
        name="ends",
    )(partial_sums, first_row, last_row)
    ends = ends.reshape(2, 2, planes, 2, 8, 16).transpose(3, 4, 0, 2, 1, 5)
    ends = ends.reshape(chips, 2, 8, 128)
    ends = jnp.take(ends, jnp.arange(chips) ^ (gx_index // 2), axis=0)
    distance = 1
    while distance < chips:
        pairs = ends.reshape(-1, 2, 2, 8, 128)
        route = [(i, i ^ (2 * distance)) for i in range(gx_count)]
        ends = pairs[:, 0] + lax.ppermute(pairs[:, 1], "gx", route)
        distance *= 2
    ends = ends.reshape(2, 8, 128)
    copies = jnp.broadcast_to(ends[None], (gy_count, 2, 8, 128))
    all_ends = lax.all_to_all(copies, "gy", split_axis=0, concat_axis=0, tiled=True)

    own_modes = lax.dynamic_slice_in_dim(mode_index, gx_index * 16, 16)
    own_modes = jnp.tile(own_modes, 8)[None, :]
    carry = pl.pallas_call(
        carry_kernel,
        out_shape=jax.ShapeDtypeStruct((6, gy_count, 8, 128), F32),
        in_specs=[SMEM, SMEM, VMEM],
        out_specs=VMEM,
        scratch_shapes=[pltpu.VMEM((4, gy_count, 8, 128), F32)],
        compiler_params=PARAMS,
        name="carry",
    )(lower_all, upper_all, own_modes)
    edges = pl.pallas_call(
        interface_kernel,
        out_shape=jax.ShapeDtypeStruct((2, 8, 128), F32),
        in_specs=[SMEM] * 3 + [VMEM] * 2,
        out_specs=VMEM,
        scratch_shapes=[
            pltpu.VMEM((gy_count, 8, 128), F32),
            pltpu.VMEM((gy_count + 1, 8, 128), F32),
        ],
        compiler_params=PARAMS,
        name="interfaces",
    )(info, lower_all, upper_all, all_ends, carry)

    column = jax.ShapeDtypeStruct((wall_rows, 8, 128), F32)
    ratio, inverse, back = pl.pallas_call(
        own_factor_kernel,
        out_shape=(column,) * 3,
        in_specs=[SMEM, SMEM, SMEM, VMEM],
        out_specs=(VMEM,) * 3,
        compiler_params=PARAMS,
        name="own_factors",
    )(info, lower_all, upper_all, own_modes)

    summed, edges, ratio = lax.optimization_barrier((summed, edges, ratio))
    return pl.pallas_call(
        solve_kernel,
        out_shape=jax.ShapeDtypeStruct((2, planes, 16, wall_rows), F32),
        in_specs=[VMEM] * 5,
        out_specs=VMEM,
        scratch_shapes=[pltpu.VMEM((planes * 32, wall_rows), F32)],
        compiler_params=PARAMS,
        name="solve",
    )(
        pltpu.with_memory_space_constraint(summed, pltpu.HBM),
        edges,
        ratio,
        inverse,
        back,
    )


def solution(mesh):
    in_specs = (P(None, "gx", "gy"), P(), P())
    out_specs = P(None, None, "gx", "gy")
    return jax.shard_map(local, mesh=mesh, in_specs=in_specs, out_specs=out_specs, check_vma=False)
```
